512 devices in a mesh: dp: 32 (over z, y_lo), ctx: 16 (over x, y_hi, core).
Axes of the slice: x: 4, y: 8 (y_hi: 2, y_lo: 4; y = y_hi * 4 + y_lo), z: 8, core: 2. Of those that a mesh axis runs over, the one named last changes fastest.
Arguments:
- frame_input: bfloat16 [64, 1024, 1536], P('dp', 'ctx'), may hold values from -6 to 6
- queries: bfloat16 [64, 1024, 768], P('dp', 'ctx'), may hold values from -18 to 18
- key_proj: bfloat16 [64, 1024, 768], P('dp', 'ctx'), may hold values from -18 to 18
- value_proj: bfloat16 [64, 1024, 768], P('dp', 'ctx'), may hold values from -6 to 6
- out_weight: bfloat16 [1536, 768], P('ctx', 'dp'), may hold values from -0.21875 to 0.21875
- conv_weight: bfloat16 [31, 1536], P(None, 'dp'), may hold values from -1 to 1
- lengths: int32 [64], P('dp'), may hold values from 256 to 1024, as said below
- grad_output: bfloat16 [64, 1024, 1536], P('dp', 'ctx'), may hold values from -6 to 6
Outputs:
- block_output: bfloat16 [64, 1024, 1536], P('dp', 'ctx')
- grad_input: bfloat16 [64, 1024, 1536], P('dp', 'ctx')
- grad_queries: bfloat16 [64, 1024, 768], P('dp', 'ctx')
- grad_keys: bfloat16 [64, 1024, 768], P('dp', 'ctx')
- grad_values: bfloat16 [64, 1024, 768], P('dp', 'ctx')
- grad_out_weight: float32 [1536, 768], P('ctx', 'dp')
- grad_conv_weight: float32 [31, 1536], P(None, 'dp')
The draws below stay inside these ranges and needn't reach their ends.
Inputs may be any that keep to these rules, and one draw needn't show every extreme that they name: `lengths`: at least one utterance of every draw fills all 1024 frame slots.
All inputs are finite; a program needn't handle non-finite values.
Results may differ from the reference program's by a relative error of at most 0.035.
Values may be sent and summed in bfloat16 or wider, within the bound.
A program may use at most 128 MiB of HBM per device.

```python
import jax
import jax.numpy as jnp
from jax import lax

UTT_DEV = 2
D = 1536
HEADS = 12
HEAD_DIM = 64
KERNEL = 31
HD = 768
FRAMES = 1024
UTTS = 64
N_DP = 32
N_CTX = 16


def draw_pairs(key):
    array_shape = (UTTS, FRAMES, HD)
    query_seed = jax.random.fold_in(key, 101)
    key_seed = jax.random.fold_in(key, 202)
    query_values = 1.7 * jnp.clip(jax.random.normal(query_seed, array_shape, jnp.float32), -6.0, 6.0)
    key_values = 1.7 * jnp.clip(jax.random.normal(key_seed, array_shape, jnp.float32), -6.0, 6.0)
    return (query_values, key_values)


def draw_queries(key, part):
    return draw_pairs(key)[0].astype(jnp.bfloat16)


def draw_key_proj(key, part):
    return draw_pairs(key)[1].astype(jnp.bfloat16)


def draw_lengths(key, part):
    drawn_lengths = jax.random.randint(jax.random.fold_in(key, 404), (UTTS,), FRAMES // 4, FRAMES + 1)
    full_index = jax.random.randint(jax.random.fold_in(key, 505), (), 0, UTTS)
    return jnp.where(jnp.arange(UTTS) == full_index, FRAMES, drawn_lengths).astype(jnp.int32)


def level_of(key, extent, cuts, least, high):
    level, own = 1.0, jax.random.fold_in(key, 6)
    for axis_at, parts in cuts:
        steps = jnp.exp(jax.random.uniform(jax.random.fold_in(own, axis_at), (parts,), jnp.float32, least / len(cuts), high / len(cuts)))
        level = level * jnp.repeat(steps, extent[axis_at] // parts).reshape([-1 if axis == axis_at else 1 for axis in range(len(extent))])
    return level


def noise(rng, shape, deviation, limit, pieces=(), kind=jnp.bfloat16):
    array = jax.random.normal(rng, shape, jnp.float32) * deviation
    if len(pieces) > 0:
        array = level_of(rng, shape, pieces, -0.22, 0.18) * array
    return jnp.clip(array, min=-limit, max=limit).astype(kind)


def setup_inputs(seed: int = 0) -> dict:
    key_list = jax.random.split(jax.random.key(seed), 9)
    frame_input = noise(key_list[0], (UTTS, FRAMES, D), 1.0, 6.0, ((0, 32), (1, 16)))
    queries = draw_queries(jax.random.fold_in(key_list[8], 71), 0)
    key_proj = draw_key_proj(jax.random.fold_in(key_list[8], 71), 0)
    value_proj = noise(key_list[3], (UTTS, FRAMES, HD), 1.0, 6.0, ((0, 32), (1, 16)))
    out_weight = noise(key_list[4], (D, HD), HD ** -0.5, 0.21875, ((0, 16), (1, 32)))
    conv_weight = noise(key_list[5], (KERNEL, D), KERNEL ** -0.5, 1.0, ((1, 32),))
    lengths = draw_lengths(jax.random.fold_in(key_list[8], 71), 0)
    grad_output = noise(key_list[7], (UTTS, FRAMES, D), 1.0, 6.0, ((0, 32), (1, 16)))
    return {"frame_input": frame_input, "queries": queries, "key_proj": key_proj, "value_proj": value_proj, "out_weight": out_weight, "conv_weight": conv_weight, "lengths": lengths, "grad_output": grad_output}


masked_score = -1e30


def rounded(values):
    return lax.optimization_barrier(values.astype(jnp.bfloat16)).astype(jnp.float32)


def one_utterance(items, out_weight, conv_weight):
    frame_input, queries, key_proj, value_proj, grad_output, length = items
    score_scale = HEAD_DIM ** -0.5
    half_span = (KERNEL - 1) // 2
    valid = jnp.arange(FRAMES, dtype=jnp.int32) < length
    query_heads = queries.astype(jnp.float32).reshape(FRAMES, HEADS, HEAD_DIM)
    key_heads = key_proj.astype(jnp.float32).reshape(FRAMES, HEADS, HEAD_DIM)
    value_heads = value_proj.astype(jnp.float32).reshape(FRAMES, HEADS, HEAD_DIM)
    scores = jnp.einsum("qhd,khd->hqk", query_heads, key_heads) * score_scale
    scores = jnp.where(valid[None, None, :], scores, masked_score)
    largest = jnp.max(scores, axis=-1, keepdims=True)
    log_total = largest + jnp.log(jnp.sum(jnp.exp(scores - largest), axis=-1, keepdims=True))
    weights = jnp.exp(scores - log_total)
    weights_low = rounded(weights)
    attended = jnp.einsum("hqk,khd->qhd", weights_low, value_heads).reshape(FRAMES, HD).astype(jnp.bfloat16)
    projected = jnp.dot(attended, out_weight.T, preferred_element_type=jnp.float32)
    hidden = (frame_input.astype(jnp.float32) + projected).astype(jnp.bfloat16)
    masked_hidden = jnp.where(valid[:, None], hidden, jnp.zeros_like(hidden))
    padded = jnp.pad(masked_hidden.astype(jnp.float32), ((half_span, half_span), (0, 0)))
    taps = conv_weight.astype(jnp.float32)
    conv_sum = taps[0] * padded[0:FRAMES]
    for tap_index in range(1, KERNEL):
        conv_sum = conv_sum + taps[tap_index] * padded[tap_index:tap_index + FRAMES]
    sigmoid = jax.nn.sigmoid(conv_sum)
    block_output = (hidden.astype(jnp.float32) + conv_sum * sigmoid).astype(jnp.bfloat16)
    swish_slope = sigmoid * (1.0 + conv_sum * (1.0 - sigmoid))
    grad_conv = (grad_output.astype(jnp.float32) * swish_slope).astype(jnp.bfloat16)
    grad_padded = jnp.pad(grad_conv.astype(jnp.float32), ((half_span, half_span), (0, 0)))
    back_sum = taps[0] * grad_padded[2 * half_span:2 * half_span + FRAMES]
    for tap_index in range(1, KERNEL):
        first_row = 2 * half_span - tap_index
        back_sum = back_sum + taps[tap_index] * grad_padded[first_row:first_row + FRAMES]
    grad_hidden = (grad_output.astype(jnp.float32) + jnp.where(valid[:, None], back_sum, 0.0)).astype(jnp.bfloat16)
    kernel_term = jnp.stack([jnp.sum(grad_conv.astype(jnp.float32) * padded[tap_index:tap_index + FRAMES], axis=0) for tap_index in range(KERNEL)])
    grad_attended = jnp.dot(grad_hidden, out_weight, preferred_element_type=jnp.float32).astype(jnp.bfloat16)
    grad_heads = grad_attended.astype(jnp.float32).reshape(FRAMES, HEADS, HEAD_DIM)
    row_delta = jnp.sum(grad_heads * attended.astype(jnp.float32).reshape(FRAMES, HEADS, HEAD_DIM), axis=-1)
    grad_weights = jnp.einsum("qhd,khd->hqk", grad_heads, value_heads)
    grad_scores = rounded(weights * (grad_weights - row_delta.T[:, :, None]))
    grad_queries = (jnp.einsum("hqk,khd->qhd", grad_scores, key_heads) * score_scale).reshape(FRAMES, HD).astype(jnp.bfloat16)
    grad_keys = (jnp.einsum("hqk,qhd->khd", grad_scores, query_heads) * score_scale).reshape(FRAMES, HD).astype(jnp.bfloat16)
    grad_values = jnp.einsum("hqk,qhd->khd", weights_low, grad_heads).reshape(FRAMES, HD).astype(jnp.bfloat16)
    return block_output, grad_hidden, grad_queries, grad_keys, grad_values, attended, kernel_term


def one_group(items, out_weight, conv_weight):
    shard_rows = FRAMES // N_CTX
    panel_sum = jnp.zeros((N_CTX, D, HD), jnp.float32)
    kernel_sum = jnp.zeros((KERNEL, D), jnp.float32)
    collected = []
    for utt_index in range(UTT_DEV):
        results = one_utterance(tuple(item[utt_index] for item in items), out_weight, conv_weight)
        hidden_blocks = results[1].astype(jnp.float32).reshape(N_CTX, shard_rows, D)
        attended_blocks = results[5].astype(jnp.float32).reshape(N_CTX, shard_rows, HD)
        panel_sum = panel_sum + jnp.einsum("cfd,cfe->cde", hidden_blocks, attended_blocks)
        kernel_sum = kernel_sum + results[6]
        collected.append(results[:5])
    stacked = tuple(jnp.stack([entry[slot] for entry in collected]) for slot in range(5))
    panel_terms = rounded(panel_sum)
    return stacked + (jnp.sum(panel_terms, axis=0), kernel_sum)


def reference(frame_input, queries, key_proj, value_proj, out_weight, conv_weight, lengths, grad_output):
    def grouped(values):
        return values.reshape((N_DP, UTT_DEV) + values.shape[1:])

    items = tuple(grouped(values) for values in (frame_input, queries, key_proj, value_proj, grad_output, lengths))
    results = lax.map(lambda group_items: one_group(group_items, out_weight, conv_weight), items)

    def flat(values):
        return values.reshape((UTTS,) + values.shape[2:])

    return (flat(results[0]), flat(results[1]), flat(results[2]), flat(results[3]), flat(results[4]),
            jnp.sum(results[5], axis=0), jnp.sum(results[6], axis=0))
```

```python
import jax
import jax.numpy as jnp
from jax import lax
from jax.experimental import pallas as pl
from jax.experimental.pallas import tpu as pltpu
from jax.sharding import PartitionSpec as P

BF = jnp.bfloat16
F32 = jnp.float32
N_CTX = 16
N_DP = 32
ROWS = 64
FRAMES = 1024
D = 1536
HD = 768
PAIRS = 6
TARGETS = 2 * PAIRS
TAPS = 31
TILE = 256
CONV_BLOCKS = D // 128
NT = (((1,), (1,)), ((), ()))
TN = (((0,), (0,)), ((), ()))


def target_of(n):
    u, p = n // PAIRS, n % PAIRS
    hi = p // 4
    x = (1 - hi) * p + hi * 2 * (p - 4)
    return 4 * x + 2 * u + hi


def remote(src, dst, send, recv, **axis):
    return pltpu.make_async_remote_copy(
        src_ref=src,
        dst_ref=dst,
        send_sem=send,
        recv_sem=recv,
        device_id=axis,
        device_id_type=pl.DeviceIdType.MESH,
    )


def arrived(dst, sem):
    pltpu.make_async_copy(dst, dst, sem).wait()


def loop(count, body):
    def step(i, carry):
        body(i)
        return carry

    lax.fori_loop(0, count, step, 0)


def mo(value, unit):
    return pl.multiple_of(value, unit)


def kernel(
    len_ref, x_ref, q_ref, k_ref, v_ref, msg_ref, go_ref,
    bo_ref, gi_ref, gq_ref, gk_ref, gv_ref, gw_ref, gt_ref,
    qkv, kx, qm, kt, vt, pt, ds, ot, ob, att_r, att, ga_s, ga_r, dqt, dbuf, grad_r,
    w_a, taps, w_full,
    hid, hb, halo, hp, gcb, ghalo, gp, tgs,
    pp, rs1, rs2s, rs2, own2, rs3s, rs3, own3, ms, mr, th, tr,
    s_p1, r_p1, s_a, r_a, s_w, r_w, s_p2, r_p2, s_h, r_h, s_p3, r_p3, s_p4, r_p4,
    s_rs1, r_rs1, s_rs2, r_rs2, s_rs3, r_rs3, s_dp, r_dp, s_t, r_t,
):
    me = lax.axis_index("ctx")
    dp = lax.axis_index("dp")
    x = me // 4
    yh = (me // 2) % 2
    core = me % 2
    sib = 4 * x + 2 * yh + (1 - core)
    ypart = 4 * x + 2 * (1 - yh) + core
    pair = (1 - core) * x + core * (4 + x // 2)
    works = (core * (x % 2)) == 0
    my_rows = pl.ds(mo(me * ROWS, ROWS), ROWS)
    inputs = (q_ref, k_ref, v_ref)

    barrier = pltpu.get_barrier_semaphore()

    def greet_ctx(i):
        @pl.when(i != me)
        def _():
            pl.semaphore_signal(barrier, inc=1, device_id={"ctx": i}, device_id_type=pl.DeviceIdType.MESH)

    def greet_dp(i):
        @pl.when(i != dp)
        def _():
            pl.semaphore_signal(barrier, inc=1, device_id={"dp": i}, device_id_type=pl.DeviceIdType.MESH)

    loop(N_CTX, greet_ctx)
    loop(N_DP, greet_dp)
    pl.semaphore_wait(barrier, N_CTX + N_DP - 2)

    def p1_parts(a, n):
        src = inputs[a].at[n // PAIRS, :, pl.ds(mo((n % PAIRS) * 128, 128), 128)]
        return src, qkv.at[a, my_rows, :]

    def p1_copy(a, n):
        src, dst = p1_parts(a, n)
        return remote(src, dst, s_p1.at[a * TARGETS + n], r_p1.at[a * N_CTX + me], ctx=target_of(n))

    def p1_start(n):
        t = target_of(n)
        for a in range(3):
            @pl.when(t != me)
            def _():
                p1_copy(a, n).start()

            @pl.when(t == me)
            def _():
                src, dst = p1_parts(a, n)
                pltpu.make_async_copy(src, dst, r_p1.at[a * N_CTX + me]).start()

    loop(TARGETS, p1_start)

    def a_copy(d):
        return remote(msg_ref, w_a.at[dp], s_a.at[d], r_a.at[dp], dp=d)

    def a_start(d):
        @pl.when(d != dp)
        def _():
            a_copy(d).start()

        @pl.when(d == dp)
        def _():
            pltpu.make_async_copy(msg_ref, w_a.at[dp], r_a.at[dp]).start()

    loop(N_DP, a_start)
    tgs[...] = jnp.zeros_like(tgs)
    own3[...] = jnp.zeros_like(own3)
    loop(N_DP, lambda d: arrived(w_a.at[d], r_a.at[d]))
    pieces = w_a[...].astype(F32)
    block = pieces[:, 0:24, :].reshape(HD, 128).T
    taps[...] = pieces.reshape(D, 128).T[96:128, :]

    def w_rows(c):
        return w_full.at[pl.ds(mo(c * 96, 32), 96), :]

    w_full[pl.ds(mo(me * 96, 32), 96), :] = block[0:96, :].astype(BF)

    def w_copy(c, slot, to):
        return remote(w_rows(c), w_rows(c), s_w.at[slot], r_w.at[c], ctx=to)

    def w_y():
        return w_copy(me, 0, ypart)

    def w_x(i, y):
        return w_copy(4 * x + 2 * y + core, 1 + 4 * y + i, 4 * i + 2 * yh + core)

    def w_sib(i):
        return w_copy(2 * i + core, 9 + i, sib)

    w_y().start()

    def w_x_start(y):
        def one(i):
            @pl.when(i != x)
            def _():
                w_x(i, y).start()

        loop(4, one)

    w_x_start(yh)

    lane = lax.broadcasted_iota(jnp.int32, (FRAMES, 128), 1)

    @pl.when(works)
    def _():
        for a in range(3):
            loop(N_CTX, lambda c: arrived(qkv.at[a, pl.ds(mo(c * ROWS, ROWS), ROWS), :], r_p1.at[a * N_CTX + c]))
        row = lax.broadcasted_iota(jnp.int32, (FRAMES, 128), 0)
        bias = jnp.where(row < len_ref[yh], 0.0, -1e30)
        q = qkv[0].astype(F32) * 0.125
        k = qkv[1].astype(F32)
        for h in range(2):
            kx[h] = jnp.where(lane == 64 * (1 - h), bias, k).astype(BF)
            mine = (lane // 64) == h
            qm[h] = jnp.where(mine, q, jnp.where(lane == 64 * (1 - h), 1.0, 0.0)).astype(BF)
        kt[...] = k.T.astype(BF)
        vt[...] = qkv[2].astype(F32).T.astype(BF)

    def forward_head(h):
        @pl.when(works)
        def _():
            def tile(i):
                cols = pl.ds(mo(i * TILE, TILE), TILE)
                s = lax.dot_general(kx[h], qm[h, cols, :], NT, preferred_element_type=F32)
                e = jnp.exp(s - jnp.max(s, axis=0, keepdims=True))
                p = (e * (1.0 / jnp.sum(e, axis=0, keepdims=True))).astype(BF)
                pt[h, :, cols] = p
                ot[64 * h:64 * h + 64, cols] = jnp.dot(
                    vt[64 * h:64 * h + 64, :], p, preferred_element_type=F32
                )

            loop(FRAMES // TILE, tile)

    forward_head(0)
    arrived(w_rows(ypart), r_w.at[ypart])
    w_x_start(1 - yh)
    forward_head(1)

    def p2_copy(c):
        rows = pl.ds(mo(c * ROWS, ROWS), ROWS)
        return remote(ob.at[rows, :], att_r.at[yh, pair], s_p2.at[c], r_p2.at[yh * PAIRS + pair], ctx=c)

    @pl.when(works)
    def _():
        ob[...] = ot[...].T.astype(BF)

        def one(c):
            @pl.when(c != me)
            def _():
                p2_copy(c).start()

            @pl.when(c == me)
            def _():
                pltpu.make_async_copy(
                    ob.at[my_rows, :], att_r.at[yh, pair], r_p2.at[yh * PAIRS + pair]
                ).start()

        loop(N_CTX, one)

    def w_forward(i):
        c = 2 * i + core

        @pl.when(((c - me) * (c - ypart)) != 0)
        def _():
            arrived(w_rows(c), r_w.at[c])

        w_sib(i).start()

    loop(8, w_forward)

    def w_last(i):
        c = 2 * i + (1 - core)
        arrived(w_rows(c), r_w.at[c])

    loop(8, w_last)
    loop(TARGETS, lambda n: arrived(att_r.at[n // PAIRS, n % PAIRS], r_p2.at[n]))
    for u in range(2):
        for p in range(PAIRS):
            att[64 * u:64 * u + 64, 128 * p:128 * p + 128] = att_r[u, p]

    frame = lax.broadcasted_iota(jnp.int32, (ROWS, TILE), 0) + me * ROWS

    def project(i):
        cols = pl.ds(mo(i * TILE, TILE), TILE)
        out = lax.dot_general(att[...], w_full[cols, :], NT, preferred_element_type=F32)
        for u in range(2):
            h = (out[64 * u:64 * u + 64, :] + x_ref[u, :, cols].astype(F32)).astype(BF).astype(F32)
            masked = jnp.where(frame < len_ref[u], h, 0.0)
            hid[u, :, cols] = h
            hb[u, :, cols] = masked.astype(BF)
            hp[u, 16:80, cols] = masked

    loop(D // TILE, project)

    def edges(src, buf, base):
        up = remote(src.at[:, 48:64, :], buf.at[0], s_h.at[base], r_h.at[base], ctx=lax.rem(me + 1, N_CTX))
        down = remote(
            src.at[:, 0:16, :], buf.at[1], s_h.at[base + 1], r_h.at[base + 1], ctx=lax.rem(me + N_CTX - 1, N_CTX)
        )
        return up, down

    def edges_start(src, buf, base):
        up, down = edges(src, buf, base)

        @pl.when(me < N_CTX - 1)
        def _():
            up.start()

        @pl.when(me > 0)
        def _():
            down.start()

    def edges_take(buf, base, padded):
        for side, first in ((0, 0), (1, 80)):
            inner = (me > 0) if side == 0 else (me < N_CTX - 1)

            @pl.when(inner)
            def _():
                arrived(buf.at[side], r_h.at[base + side])
                padded[:, first:first + 16, :] = buf[side].astype(F32)

            @pl.when(jnp.logical_not(inner))
            def _():
                padded[:, first:first + 16, :] = jnp.zeros((2, 16, D), F32)

    def rolled_by(block, r):
        return block if r == 0 else pltpu.roll(block, 96 - r, 0)

    edges_start(hb, halo, 0)
    edges_take(halo, 0, hp)

    def conv_forward(i):
        cols = pl.ds(mo(i * 128, 128), 128)
        w = taps[:, cols]
        for u in range(2):
            block = hp[u, :, cols]
            acc = jnp.zeros((ROWS, 128), F32)
            for r in range(8):
                moved = rolled_by(block, r)
                for a in range(4):
                    j = 8 * a + r - 1
                    if 0 <= j < TAPS:
                        acc = acc + w[j:j + 1, :] * moved[8 * a:8 * a + ROWS, :]
            sg = jax.nn.sigmoid(acc)
            bo_ref[u, :, cols] = (hid[u, :, cols] + acc * sg).astype(BF)
            gc = (go_ref[u, :, cols].astype(F32) * (sg * (1.0 + acc * (1.0 - sg)))).astype(BF)
            gcb[u, :, cols] = gc
            gp[u, 16:80, cols] = gc.astype(F32)

    loop(CONV_BLOCKS, conv_forward)
    edges_start(gcb, ghalo, 2)

    def taps_gradient(i):
        cols = pl.ds(mo(i * 128, 128), 128)
        blocks = [hp[u, :, cols] for u in range(2)]
        grads = [gp[u, 16:80, cols] for u in range(2)]
        for r in range(8):
            moved = [rolled_by(block, r) for block in blocks]
            for a in range(4):
                j = 8 * a + r - 1
                if 0 <= j < TAPS:
                    total = sum(g * m[8 * a:8 * a + ROWS, :] for g, m in zip(grads, moved))
                    tgs[96 + j:97 + j, cols] = jnp.sum(total, axis=0, keepdims=True)

    loop(CONV_BLOCKS, taps_gradient)
    edges_take(ghalo, 2, gp)
    frame_c = lax.broadcasted_iota(jnp.int32, (ROWS, 128), 0) + me * ROWS

    def conv_backward(i):
        cols = pl.ds(mo(i * 128, 128), 128)
        w = taps[:, cols]
        for u in range(2):
            block = gp[u, :, cols]
            acc = jnp.zeros((ROWS, 128), F32)
            for r in range(8):
                moved = rolled_by(block, r)
                for a in range(4):
                    j = 31 - (8 * a + r)
                    if 0 <= j < TAPS:
                        acc = acc + w[j:j + 1, :] * moved[8 * a:8 * a + ROWS, :]
            gi = go_ref[u, :, cols].astype(F32) + jnp.where(frame_c < len_ref[u], acc, 0.0)
            gi_ref[u, :, cols] = gi.astype(BF)

    loop(CONV_BLOCKS, conv_backward)

    def p3_copy(n):
        return remote(
            ga_s.at[n // PAIRS, n % PAIRS], ga_r.at[my_rows, :], s_p3.at[n], r_p3.at[me], ctx=target_of(n)
        )

    gi_rows = gi_ref[...].reshape(2 * ROWS, D)
    for part in range(HD // TILE):
        out = jnp.dot(gi_rows, w_full[:, TILE * part:TILE * part + TILE], preferred_element_type=F32).astype(BF)
        for u in range(2):
            for half in range(2):
                ga_s[u, 2 * part + half] = out[64 * u:64 * u + 64, 128 * half:128 * half + 128]

    def p3_start(n):
        t = target_of(n)

        @pl.when(t != me)
        def _():
            p3_copy(n).start()

        @pl.when(t == me)
        def _():
            pltpu.make_async_copy(ga_s.at[n // PAIRS, n % PAIRS], ga_r.at[my_rows, :], r_p3.at[me]).start()

    loop(TARGETS, p3_start)

    def rs1_copy(i):
        return remote(
            pp.at[pl.ds(2 * i, 2), 1 - core], rs1.at[pl.ds(2 * i, 2)], s_rs1.at[i], r_rs1.at[i], ctx=sib
        )

    def panel(i):
        cols = pl.ds(mo(i * 384, 128), 384)
        gi_cols = jnp.concatenate([gi_ref[0, :, cols], gi_ref[1, :, cols]], axis=0)
        out = lax.dot_general(gi_cols, att[...], TN, preferred_element_type=F32)
        pp[pl.ds(2 * i, 2)] = out.reshape(2, 2, 96, HD).astype(BF)
        rs1_copy(i).start()

    loop(4, panel)

    def rs2_copy(i):
        return remote(rs2s.at[i], rs2.at[x], s_rs2.at[i], r_rs2.at[x], ctx=4 * i + 2 * yh + core)

    def rs2_start(i):
        two = pl.ds(2 * i, 2)
        arrived(rs1.at[two], r_rs1.at[i])
        total = pp[two, core].astype(F32) + rs1[two].astype(F32)

        @pl.when(i != x)
        def _():
            rs2s[i] = total.astype(BF)
            rs2_copy(i).start()

        @pl.when(i == x)
        def _():
            own2[...] = total

    loop(4, rs2_start)

    @pl.when(works)
    def _():
        loop(N_CTX, lambda c: arrived(ga_r.at[pl.ds(mo(c * ROWS, ROWS), ROWS), :], r_p3.at[c]))

    def backward_head(h):
        @pl.when(works)
        def _():
            def tile(i):
                cols = pl.ds(mo(i * TILE, TILE), TILE)
                mine = (lax.broadcasted_iota(jnp.int32, (TILE, 128), 1) // 64) == h
                ga = ga_r[cols, :].astype(F32)
                gm = jnp.where(mine, ga, 0.0)
                prod = gm * ob[cols, :].astype(F32)
                delta = jnp.sum(prod.T, axis=0, keepdims=True)
                gmb = gm.astype(BF)
                dpt = lax.dot_general(qkv[2], gmb, NT, preferred_element_type=F32)
                dst = (pt[h, :, cols].astype(F32) * (dpt - delta)).astype(BF)
                ds[h, :, cols] = dst
                dqt[64 * h:64 * h + 64, cols] = jnp.dot(
                    kt[64 * h:64 * h + 64, :], dst, preferred_element_type=F32
                )

            loop(FRAMES // TILE, tile)

    backward_head(0)

    def rs2_take(i):
        @pl.when(i != x)
        def _():
            arrived(rs2.at[i], r_rs2.at[i])
            own2[...] += rs2[i].astype(F32)

    def rs3_copy():
        return remote(rs3s, rs3, s_rs3, r_rs3, ctx=ypart)

    loop(4, rs2_take)
    rs3s[...] = own2[1 - yh].astype(BF)
    rs3_copy().start()
    backward_head(1)

    def p4_copy(a, c):
        rows = pl.ds(mo(c * ROWS, ROWS), ROWS)
        return remote(
            dbuf.at[a, rows, :], grad_r.at[a, yh, pair], s_p4.at[a * N_CTX + c],
            r_p4.at[a * TARGETS + yh * PAIRS + pair], ctx=c,
        )

    def p4_start(a):
        def one(c):
            @pl.when(c != me)
            def _():
                p4_copy(a, c).start()

            @pl.when(c == me)
            def _():
                pltpu.make_async_copy(
                    dbuf.at[a, my_rows, :], grad_r.at[a, yh, pair], r_p4.at[a * TARGETS + yh * PAIRS + pair]
                ).start()

        loop(N_CTX, one)

    @pl.when(works)
    def _():
        dbuf[0] = (dqt[...].T * 0.125).astype(BF)
        p4_start(0)
        mine = (lane // 64) == 0
        qs = [jnp.where((lane // 64) == h, qkv[0].astype(F32) * 0.125, 0.0).astype(BF) for h in range(2)]
        for h in range(2):
            qm[h] = qs[h]

        def keys(i):
            rows = pl.ds(mo(i * TILE, TILE), TILE)
            out = jnp.dot(ds[0, rows, :], qm[0], preferred_element_type=F32)
            out = out + jnp.dot(ds[1, rows, :], qm[1], preferred_element_type=F32)
            dbuf[1, rows, :] = out.astype(BF)

        loop(FRAMES // TILE, keys)
        p4_start(1)

        def values(i):
            rows = pl.ds(mo(i * TILE, TILE), TILE)
            first = jnp.dot(pt[0, rows, :], ga_r[...], preferred_element_type=F32)
            second = jnp.dot(pt[1, rows, :], ga_r[...], preferred_element_type=F32)
            low = (lax.broadcasted_iota(jnp.int32, (TILE, 128), 1) // 64) == 0
            dbuf[2, rows, :] = jnp.where(low, first, second).astype(BF)

        loop(FRAMES // TILE, values)
        p4_start(2)

    arrived(rs3, r_rs3)
    own3[0:96, :] = own2[yh] + rs3[...].astype(F32)
    columns = own3[...].T.reshape(N_DP, 24, 128)
    tap_rows = tgs[...].T.reshape(N_DP, 48, 128)
    joined = jnp.concatenate([tap_rows[:, 0:24, :] + columns, tap_rows[:, 24:48, :]], axis=1)
    ms[...] = joined.astype(BF)

    def dp_copy(d):
        return remote(ms.at[d], mr.at[dp], s_dp.at[d], r_dp.at[dp], dp=d)

    def dp_start(d):
        @pl.when(d != dp)
        def _():
            dp_copy(d).start()

        @pl.when(d == dp)
        def _():
            pltpu.make_async_copy(ms.at[d], mr.at[dp], r_dp.at[dp]).start()

    loop(N_DP, dp_start)
    loop(N_DP, lambda d: arrived(mr.at[d], r_dp.at[d]))
    total = jnp.sum(mr[...].astype(F32), axis=0)
    gw_ref[...] = total
    th[...] = total.astype(BF)

    def t_copy(c):
        return remote(th, tr.at[me], s_t.at[c], r_t.at[me], ctx=c)

    def t_start(c):
        @pl.when(c != me)
        def _():
            t_copy(c).start()

        @pl.when(c == me)
        def _():
            pltpu.make_async_copy(th, tr.at[me], r_t.at[me]).start()

    loop(N_CTX, t_start)

    def p4_take(a):
        loop(TARGETS, lambda n: arrived(grad_r.at[a, n // PAIRS, n % PAIRS], r_p4.at[a * TARGETS + n]))

    for a, out in ((0, gq_ref), (1, gk_ref), (2, gv_ref)):
        p4_take(a)
        for u in range(2):
            for p in range(PAIRS):
                out[u, :, 128 * p:128 * p + 128] = grad_r[a, u, p]

    loop(N_CTX, lambda c: arrived(tr.at[c], r_t.at[c]))
    gt_ref[...] = jnp.sum(tr[...].astype(F32), axis=0)

    def sent(n):
        @pl.when(target_of(n) != me)
        def _():
            for a in range(3):
                p1_copy(a, n).wait_send()
            p3_copy(n).wait_send()

    loop(TARGETS, sent)

    def sent_dp(d):
        @pl.when(d != dp)
        def _():
            a_copy(d).wait_send()
            dp_copy(d).wait_send()

    loop(N_DP, sent_dp)

    def sent_ctx(c):
        @pl.when(c != me)
        def _():
            t_copy(c).wait_send()

            @pl.when(works)
            def _():
                p2_copy(c).wait_send()
                for a in range(3):
                    p4_copy(a, c).wait_send()

    loop(N_CTX, sent_ctx)
    w_y().wait_send()

    def sent_x(i):
        @pl.when(i != x)
        def _():
            w_x(i, 0).wait_send()
            w_x(i, 1).wait_send()
            rs2_copy(i).wait_send()

        rs1_copy(i).wait_send()

    loop(4, sent_x)
    loop(8, lambda i: w_sib(i).wait_send())
    rs3_copy().wait_send()
    for src, buf, base in ((hb, halo, 0), (gcb, ghalo, 2)):
        up, down = edges(src, buf, base)

        @pl.when(me < N_CTX - 1)
        def _():
            up.wait_send()

        @pl.when(me > 0)
        def _():
            down.wait_send()


def per_device(frame_input, queries, key_proj, value_proj, out_weight, conv_weight, lengths, grad_output):
    left = jnp.pad(out_weight.T, ((0, 24), (0, 0)))
    right = jnp.pad(conv_weight.T, ((0, 0), (0, 1)))
    message = jnp.concatenate([left, right], axis=1)
    vmem = pl.BlockSpec(memory_space=pltpu.VMEM)
    dma = lambda n: pltpu.SemaphoreType.DMA((n,))
    scratch = [
        ((3, FRAMES, 128), BF), ((2, FRAMES, 128), BF), ((2, FRAMES, 128), BF), ((128, FRAMES), BF),
        ((128, FRAMES), BF), ((2, FRAMES, FRAMES), BF), ((2, FRAMES, FRAMES), BF), ((128, FRAMES), F32),
        ((FRAMES, 128), BF), ((2, PAIRS, ROWS, 128), BF), ((2 * ROWS, HD), BF), ((2, PAIRS, ROWS, 128), BF),
        ((FRAMES, 128), BF), ((128, FRAMES), F32), ((3, FRAMES, 128), BF), ((3, 2, PAIRS, ROWS, 128), BF),
        ((N_DP, 48, 128), BF), ((32, D), F32), ((D, HD), BF),
        ((2, ROWS, D), F32), ((2, ROWS, D), BF), ((2, 2, 16, D), BF), ((2, 96, D), F32),
        ((2, ROWS, D), BF), ((2, 2, 16, D), BF), ((2, 96, D), F32), ((128, D), F32),
        ((8, 2, 96, HD), BF), ((8, 96, HD), BF), ((4, 2, 96, HD), BF), ((4, 2, 96, HD), BF),
        ((2, 96, HD), F32), ((96, HD), BF), ((96, HD), BF), ((128, HD), F32),
        ((N_DP, 48, 128), BF), ((N_DP, 48, 128), BF), ((48, 128), BF), ((N_CTX, 48, 128), BF),
    ]
    one = pltpu.SemaphoreType.DMA
    sems = [
        dma(36), dma(48), dma(32), dma(32), dma(17), dma(16), dma(16), dma(12), dma(4), dma(4), dma(12), dma(16),
        dma(48), dma(36), dma(4), dma(4), dma(4), dma(4), one, one, dma(32), dma(32), dma(16), dma(16),
    ]
    shapes = (
        ((2, ROWS, D), BF), ((2, ROWS, D), BF), ((2, ROWS, HD), BF), ((2, ROWS, HD), BF), ((2, ROWS, HD), BF),
        ((48, 128), F32), ((48, 128), F32),
    )
    bo, gi, gq, gk, gv, gw, gt = pl.pallas_call(
        kernel,
        out_shape=[jax.ShapeDtypeStruct(s, t) for s, t in shapes],
        in_specs=[pl.BlockSpec(memory_space=pltpu.SMEM)] + [vmem] * 6,
        out_specs=[vmem] * 7,
        scratch_shapes=[pltpu.VMEM(s, t) for s, t in scratch] + sems,
        compiler_params=pltpu.CompilerParams(
            collective_id=0, has_side_effects=True, vmem_limit_bytes=50 * 1024 * 1024
        ),
        cost_estimate=pl.CostEstimate(flops=3 * 10**9, bytes_accessed=4 * 10**6, transcendentals=2 * 10**6),
    )(lengths, frame_input, queries, key_proj, value_proj, message, grad_output)
    return bo, gi, gq, gk, gv, gw[0:24, 0:96].T, gt[:, 96:96 + TAPS].T


def solution(mesh):
    rows = P("dp", "ctx", None)
    return jax.shard_map(
        per_device,
        mesh=mesh,
        in_specs=(rows, rows, rows, rows, P("ctx", "dp"), P(None, "dp"), P("dp"), rows),
        out_specs=(rows, rows, rows, rows, rows, P("ctx", "dp"), P(None, "dp")),
        check_vma=False,
    )
```

```python
import jax
import jax.numpy as jnp
from jax import lax
from jax.experimental import pallas as pl
from jax.experimental.pallas import tpu as pltpu
from jax.sharding import PartitionSpec as P

BF = jnp.bfloat16
F32 = jnp.float32
N_CTX = 16
N_DP = 32
ROWS = 64
FRAMES = 1024
D = 1536
HD = 768
PAIRS = 6
TARGETS = 2 * PAIRS
TAPS = 31
TILE = 256
CONV_BLOCKS = D // 128
NT = (((1,), (1,)), ((), ()))
TN = (((0,), (0,)), ((), ()))


def target_of(n):
    u, p = n // PAIRS, n % PAIRS
    hi = p // 4
    x = (1 - hi) * p + hi * 2 * (p - 4)
    return 4 * x + 2 * u + hi


def remote(src, dst, send, recv, **axis):
    return pltpu.make_async_remote_copy(
        src_ref=src,
        dst_ref=dst,
        send_sem=send,
        recv_sem=recv,
        device_id=axis,
        device_id_type=pl.DeviceIdType.MESH,
    )


def arrived(dst, sem):
    pltpu.make_async_copy(dst, dst, sem).wait()


def loop(count, body):
    def step(i, carry):
        body(i)
        return carry

    lax.fori_loop(0, count, step, 0)


def mo(value, unit):
    return pl.multiple_of(value, unit)


def kernel(
    len_ref, x_ref, q_ref, k_ref, v_ref, msg_ref, go_ref,
    bo_ref, gi_ref, gq_ref, gk_ref, gv_ref, gw_ref, gt_ref,
    x_v, go_v, qkv, kx, qm, kt, vt, pt, ds, ob, att_r, att, ga_s, ga_r, dbuf, grad_r,
    w_a, taps, w_full,
    hid, hb, halo, hp, gcb, ghalo, gp, tgs,
    pp, rs1, rs2s, rs2, own2, rs3s, rs3, own3, ms, mr, tms, tmr, th, tr,
    s_in, s_p1, r_p1, s_a, r_a, s_w, r_w, s_p2, r_p2, s_h, r_h, s_p3, r_p3, s_p4, r_p4,
    s_rs1, r_rs1, s_rs2, r_rs2, s_rs3, r_rs3, s_dp, r_dp, s_td, r_td, s_t, r_t,
):
    me = lax.axis_index("ctx")
    dp = lax.axis_index("dp")
    x = me // 4
    yh = (me // 2) % 2
    core = me % 2
    sib = 4 * x + 2 * yh + (1 - core)
    ypart = 4 * x + 2 * (1 - yh) + core
    pair = (1 - core) * x + core * (4 + x // 2)
    works = (core * (x % 2)) == 0
    my_rows = pl.ds(mo(me * ROWS, ROWS), ROWS)
    inputs = (q_ref, k_ref, v_ref)

    loads = [pltpu.make_async_copy(a, b, s_in.at[i]) for i, (a, b) in enumerate(((x_ref, x_v), (go_ref, go_v)))]
    for load in loads:
        load.start()

    barrier = pltpu.get_barrier_semaphore()

    def greet_ctx(i):
        @pl.when(i != me)
        def _():
            pl.semaphore_signal(barrier, inc=1, device_id={"ctx": i}, device_id_type=pl.DeviceIdType.MESH)

    def greet_dp(i):
        @pl.when(i != dp)
        def _():
            pl.semaphore_signal(barrier, inc=1, device_id={"dp": i}, device_id_type=pl.DeviceIdType.MESH)

    loop(N_CTX, greet_ctx)
    loop(N_DP, greet_dp)
    pl.semaphore_wait(barrier, N_CTX + N_DP - 2)

    def p1_parts(a, n):
        src = inputs[a].at[n // PAIRS, :, pl.ds(mo((n % PAIRS) * 128, 128), 128)]
        return src, qkv.at[a, my_rows, :]

    def p1_copy(a, n):
        src, dst = p1_parts(a, n)
        return remote(src, dst, s_p1.at[a * TARGETS + n], r_p1.at[a * N_CTX + me], ctx=target_of(n))

    def p1_start(a):
        def one(i):
            n = lax.rem(i + me, TARGETS)
            t = target_of(n)

            @pl.when(t != me)
            def _():
                p1_copy(a, n).start()

            @pl.when(t == me)
            def _():
                src, dst = p1_parts(a, n)
                pltpu.make_async_copy(src, dst, r_p1.at[a * N_CTX + me]).start()

        loop(TARGETS, one)

    def a_copy(d):
        return remote(msg_ref, w_a.at[dp], s_a.at[d], r_a.at[dp], dp=d)

    def a_start(i):
        a_copy(lax.rem(i + 1 + dp, N_DP)).start()

    loop(N_DP - 1, a_start)
    pltpu.make_async_copy(msg_ref, w_a.at[dp], r_a.at[dp]).start()
    p1_start(1)
    p1_start(0)
    p1_start(2)
    tgs[...] = jnp.zeros_like(tgs)
    own3[...] = jnp.zeros_like(own3)
    loop(N_DP, lambda d: arrived(w_a.at[d], r_a.at[d]))
    pieces = w_a[...].astype(F32)
    block = pieces[:, 0:24, :].reshape(HD, 128).T
    rest = pieces[:, 24:32, :].reshape(N_DP * 8, 128)
    moved_rest = [pltpu.roll(rest, 96 - 32 * k, 1).reshape(N_DP, 8, 128) for k in range(3)]
    taps[...] = jnp.concatenate([pieces[:, 0:24, :]] + moved_rest, axis=1).reshape(D, 128).T[96:128, :]

    def w_rows(c):
        return w_full.at[pl.ds(mo(c * 96, 32), 96), :]

    w_full[pl.ds(mo(me * 96, 32), 96), :] = block[0:96, :].astype(BF)

    def w_copy(c, slot, to):
        return remote(w_rows(c), w_rows(c), s_w.at[slot], r_w.at[c], ctx=to)

    def w_y():
        return w_copy(me, 0, ypart)

    def w_x(i, y):
        return w_copy(4 * x + 2 * y + core, 1 + 4 * y + i, 4 * i + 2 * yh + core)

    def w_sib(i):
        return w_copy(2 * i + core, 9 + i, sib)

    w_y().start()

    def w_x_start(y):
        def one(i):
            @pl.when(i != x)
            def _():
                w_x(i, y).start()

        loop(4, one)

    w_x_start(yh)

    lane = lax.broadcasted_iota(jnp.int32, (FRAMES, 128), 1)

    def p1_take(a):
        loop(N_CTX, lambda c: arrived(qkv.at[a, pl.ds(mo(c * ROWS, ROWS), ROWS), :], r_p1.at[a * N_CTX + c]))

    @pl.when(works)
    def _():
        p1_take(1)
        row = lax.broadcasted_iota(jnp.int32, (FRAMES, 128), 0)
        bias = jnp.where(row < len_ref[yh], 0.0, -1e30)
        k = qkv[1].astype(F32)
        for h in range(2):
            kx[h] = jnp.where(lane == 64 * (1 - h), bias, k).astype(BF)
        kt[...] = k.T.astype(BF)
        p1_take(0)
        q = qkv[0].astype(F32) * 0.125
        for h in range(2):
            mine = (lane // 64) == h
            qm[h] = jnp.where(mine, q, jnp.where(lane == 64 * (1 - h), 1.0, 0.0)).astype(BF)

    def weights_of(h):
        @pl.when(works)
        def _():
            def tile(i):
                cols = pl.ds(mo(i * TILE, TILE), TILE)
                s = lax.dot_general(kx[h], qm[h, cols, :], NT, preferred_element_type=F32)
                e = jnp.exp(s - jnp.max(s, axis=0, keepdims=True))
                pt[h, :, cols] = (e * (1.0 / jnp.sum(e, axis=0, keepdims=True))).astype(BF)

            loop(FRAMES // TILE, tile)

    weights_of(0)
    arrived(w_rows(ypart), r_w.at[ypart])
    w_x_start(1 - yh)
    weights_of(1)

    def p2_copy(c):
        rows = pl.ds(mo(c * ROWS, ROWS), ROWS)
        return remote(ob.at[rows, :], att_r.at[yh, pair], s_p2.at[c], r_p2.at[yh * PAIRS + pair], ctx=c)

    def p2_start(c):
        @pl.when(c != me)
        def _():
            p2_copy(c).start()

        @pl.when(c == me)
        def _():
            pltpu.make_async_copy(ob.at[my_rows, :], att_r.at[yh, pair], r_p2.at[yh * PAIRS + pair]).start()

    @pl.when(works)
    def _():
        p1_take(2)
        vt[...] = qkv[2].astype(F32).T.astype(BF)

        def tile(i):
            cols = pl.ds(mo(i * TILE, TILE), TILE)
            out = [
                jnp.dot(vt[64 * h:64 * h + 64, :], pt[h, :, cols], preferred_element_type=F32) for h in range(2)
            ]
            ob[cols, :] = jnp.concatenate(out, axis=0).T.astype(BF)
            loop(TILE // ROWS, lambda j: p2_start(i * (TILE // ROWS) + j))

        loop(FRAMES // TILE, tile)

    def w_forward(i):
        c = 2 * i + core

        @pl.when(((c - me) * (c - ypart)) != 0)
        def _():
            arrived(w_rows(c), r_w.at[c])

        w_sib(i).start()

    loop(8, w_forward)

    def w_last(i):
        c = 2 * i + (1 - core)
        arrived(w_rows(c), r_w.at[c])

    loop(8, w_last)
    loop(TARGETS, lambda n: arrived(att_r.at[n // PAIRS, n % PAIRS], r_p2.at[n]))
    for u in range(2):
        for p in range(PAIRS):
            att[64 * u:64 * u + 64, 128 * p:128 * p + 128] = att_r[u, p]

    frame = lax.broadcasted_iota(jnp.int32, (ROWS, TILE), 0) + me * ROWS
    before, after = me > 0, me < N_CTX - 1
    col_tiles = D // TILE

    def edge_copies(src, buf, base, i):
        cols = pl.ds(mo(i * TILE, TILE), TILE)
        up = remote(
            src.at[:, 48:64, cols], buf.at[0, :, :, cols], s_h.at[base + i], r_h.at[base + i],
            ctx=lax.rem(me + 1, N_CTX),
        )
        down = remote(
            src.at[:, 0:16, cols], buf.at[1, :, :, cols], s_h.at[base + 6 + i], r_h.at[base + 6 + i],
            ctx=lax.rem(me + N_CTX - 1, N_CTX),
        )
        return up, down

    def edges_do(src, buf, base, i, what):
        up, down = edge_copies(src, buf, base, i)

        @pl.when(after)
        def _():
            what(up)

        @pl.when(before)
        def _():
            what(down)

    def edges_take(buf, base, padded, i):
        cols = pl.ds(mo(i * TILE, TILE), TILE)
        for side, first, inner in ((0, 0, before), (1, 80, after)):
            @pl.when(inner)
            def _():
                arrived(buf.at[side, :, :, cols], r_h.at[base + 6 * side + i])
                padded[:, first:first + 16, cols] = buf[side, :, :, cols].astype(F32)

            @pl.when(jnp.logical_not(inner))
            def _():
                padded[:, first:first + 16, cols] = jnp.zeros((2, 16, TILE), F32)

    def rolled_by(block, r):
        return block if r == 0 else pltpu.roll(block, 96 - r, 0)

    for load in loads:
        load.wait()

    def project(i):
        cols = pl.ds(mo(i * TILE, TILE), TILE)
        out = lax.dot_general(att[...], w_full[cols, :], NT, preferred_element_type=F32)
        for u in range(2):
            h = (out[64 * u:64 * u + 64, :] + x_v[u, :, cols].astype(F32)).astype(BF).astype(F32)
            masked = jnp.where(frame < len_ref[u], h, 0.0)
            hid[u, :, cols] = h
            hb[u, :, cols] = masked.astype(BF)
            hp[u, 16:80, cols] = masked
        edges_do(hb, halo, 0, i, lambda copy: copy.start())

    loop(col_tiles, project)

    def conv_forward(i):
        edges_take(halo, 0, hp, i)
        for half in range(2):
            cols = pl.ds(mo(i * TILE + half * 128, 128), 128)
            w = taps[:, cols]
            for u in range(2):
                block = hp[u, :, cols]
                acc = jnp.zeros((ROWS, 128), F32)
                for r in range(8):
                    moved = rolled_by(block, r)
                    for a in range(4):
                        j = 8 * a + r - 1
                        if 0 <= j < TAPS:
                            acc = acc + w[j:j + 1, :] * moved[8 * a:8 * a + ROWS, :]
                sg = jax.nn.sigmoid(acc)
                bo_ref[u, :, cols] = (hid[u, :, cols] + acc * sg).astype(BF)
                gc = (go_v[u, :, cols].astype(F32) * (sg * (1.0 + acc * (1.0 - sg)))).astype(BF)
                gcb[u, :, cols] = gc
                gp[u, 16:80, cols] = gc.astype(F32)
        edges_do(gcb, ghalo, 12, i, lambda copy: copy.start())

    loop(col_tiles, conv_forward)

    def taps_gradient(i):
        cols = pl.ds(mo(i * 128, 128), 128)
        blocks = [hp[u, :, cols] for u in range(2)]
        grads = [gp[u, 16:80, cols] for u in range(2)]
        for r in range(8):
            moved = [rolled_by(block, r) for block in blocks]
            for a in range(4):
                j = 8 * a + r - 1
                if 0 <= j < TAPS:
                    total = sum(g * m[8 * a:8 * a + ROWS, :] for g, m in zip(grads, moved))
                    tgs[j:j + 1, cols] = jnp.sum(total, axis=0, keepdims=True)

    loop(CONV_BLOCKS, taps_gradient)
    frame_c = lax.broadcasted_iota(jnp.int32, (ROWS, 128), 0) + me * ROWS

    def conv_backward(i):
        edges_take(ghalo, 12, gp, i)
        for half in range(2):
            cols = pl.ds(mo(i * TILE + half * 128, 128), 128)
            w = taps[:, cols]
            for u in range(2):
                block = gp[u, :, cols]
                acc = jnp.zeros((ROWS, 128), F32)
                for r in range(8):
                    moved = rolled_by(block, r)
                    for a in range(4):
                        j = 31 - (8 * a + r)
                        if 0 <= j < TAPS:
                            acc = acc + w[j:j + 1, :] * moved[8 * a:8 * a + ROWS, :]
                gi = go_v[u, :, cols].astype(F32) + jnp.where(frame_c < len_ref[u], acc, 0.0)
                gi_ref[u, :, cols] = gi.astype(BF)

    loop(col_tiles, conv_backward)

    def p3_copy(n):
        return remote(
            ga_s.at[n // PAIRS, n % PAIRS], ga_r.at[my_rows, :], s_p3.at[n], r_p3.at[me], ctx=target_of(n)
        )

    gi_rows = gi_ref[...].reshape(2 * ROWS, D)

    def p3_start(n):
        t = target_of(n)

        @pl.when(t != me)
        def _():
            p3_copy(n).start()

        @pl.when(t == me)
        def _():
            pltpu.make_async_copy(ga_s.at[n // PAIRS, n % PAIRS], ga_r.at[my_rows, :], r_p3.at[me]).start()

    def cotangent(i):
        cols = pl.ds(mo(i * TILE, TILE), TILE)
        out = jnp.dot(gi_rows, w_full[:, cols], preferred_element_type=F32).astype(BF)
        for u in range(2):
            for half in range(2):
                ga_s[u, 2 * i + half] = out[64 * u:64 * u + 64, 128 * half:128 * half + 128]
        loop(4, lambda m: p3_start((m // 2) * PAIRS + 2 * i + m % 2))

    loop(HD // TILE, cotangent)

    tap_rows = tgs[...].T.reshape(N_DP, 48, 128)
    packed = [tap_rows[:, 0:16, :]] + [
        pltpu.roll(tap_rows[:, 16 * k:16 * k + 16, :].reshape(N_DP * 16, 128), 32 * k, 1).reshape(N_DP, 16, 128)
        for k in (1, 2)
    ]
    tms[...] = (packed[0] + packed[1] + packed[2]).astype(BF)

    def dp_all(src, dst, send, recv):
        def copy(d):
            return remote(src.at[d], dst.at[dp], send.at[d], recv.at[dp], dp=d)

        def start(i):
            copy(lax.rem(i + 1 + dp, N_DP)).start()

        def go():
            loop(N_DP - 1, start)
            pltpu.make_async_copy(src.at[dp], dst.at[dp], recv.at[dp]).start()

        return copy, go

    td_copy, td_start = dp_all(tms, tmr, s_td, r_td)
    dp_copy, dp_start = dp_all(ms, mr, s_dp, r_dp)
    def rs1_copy(i):
        return remote(
            pp.at[pl.ds(2 * i, 2), 1 - core], rs1.at[pl.ds(2 * i, 2)], s_rs1.at[i], r_rs1.at[i], ctx=sib
        )

    def panel(i):
        cols = pl.ds(mo(i * 384, 128), 384)
        gi_cols = jnp.concatenate([gi_ref[0, :, cols], gi_ref[1, :, cols]], axis=0)
        out = lax.dot_general(gi_cols, att[...], TN, preferred_element_type=F32)
        pp[pl.ds(2 * i, 2)] = out.reshape(2, 2, 96, HD).astype(BF)
        rs1_copy(i).start()

    loop(4, panel)
    td_start()

    def rs2_copy(i):
        return remote(rs2s.at[i], rs2.at[x], s_rs2.at[i], r_rs2.at[x], ctx=4 * i + 2 * yh + core)

    def rs2_start(i):
        two = pl.ds(2 * i, 2)
        arrived(rs1.at[two], r_rs1.at[i])
        total = pp[two, core].astype(F32) + rs1[two].astype(F32)

        @pl.when(i != x)
        def _():
            rs2s[i] = total.astype(BF)
            rs2_copy(i).start()

        @pl.when(i == x)
        def _():
            own2[...] = total

    loop(4, rs2_start)

    def p4_copy(a, c):
        rows = pl.ds(mo(c * ROWS, ROWS), ROWS)
        return remote(
            dbuf.at[a, rows, :], grad_r.at[a, yh, pair], s_p4.at[a * N_CTX + c],
            r_p4.at[a * TARGETS + yh * PAIRS + pair], ctx=c,
        )

    def p4_start(a, i):
        def one(j):
            c = i * (TILE // ROWS) + j

            @pl.when(c != me)
            def _():
                p4_copy(a, c).start()

            @pl.when(c == me)
            def _():
                pltpu.make_async_copy(
                    dbuf.at[a, my_rows, :], grad_r.at[a, yh, pair], r_p4.at[a * TARGETS + yh * PAIRS + pair]
                ).start()

        loop(TILE // ROWS, one)

    tile_lane = lax.broadcasted_iota(jnp.int32, (TILE, 128), 1) // 64

    @pl.when(works)
    def _():
        loop(N_CTX, lambda c: arrived(ga_r.at[pl.ds(mo(c * ROWS, ROWS), ROWS), :], r_p3.at[c]))

        def values(i):
            rows = pl.ds(mo(i * TILE, TILE), TILE)
            first = jnp.dot(pt[0, rows, :], ga_r[...], preferred_element_type=F32)
            second = jnp.dot(pt[1, rows, :], ga_r[...], preferred_element_type=F32)
            dbuf[2, rows, :] = jnp.where(tile_lane == 0, first, second).astype(BF)
            p4_start(2, i)

        loop(FRAMES // TILE, values)

    def backward_tile(i):
        cols = pl.ds(mo(i * TILE, TILE), TILE)
        ga = ga_r[cols, :].astype(F32)
        prod = (ga * ob[cols, :].astype(F32)).T
        parts = []
        for h in range(2):
            gmb = jnp.where(tile_lane == h, ga, 0.0).astype(BF)
            delta = jnp.sum(prod[64 * h:64 * h + 64, :], axis=0, keepdims=True)
            dpt = lax.dot_general(qkv[2], gmb, NT, preferred_element_type=F32)
            dst = (pt[h, :, cols].astype(F32) * (dpt - delta)).astype(BF)
            ds[h, :, cols] = dst
            parts.append(jnp.dot(kt[64 * h:64 * h + 64, :], dst, preferred_element_type=F32))
        dbuf[0, cols, :] = (jnp.concatenate(parts, axis=0).T * 0.125).astype(BF)
        p4_start(0, i)

    def backward_half(first):
        @pl.when(works)
        def _():
            loop(2, lambda i: backward_tile(i + first))

    backward_half(0)

    def t_copy(c):
        return remote(th, tr.at[me], s_t.at[c], r_t.at[me], ctx=c)

    def t_start(i):
        t_copy(lax.rem(i + 1 + me, N_CTX)).start()

    loop(N_DP, lambda d: arrived(tmr.at[d], r_td.at[d]))
    th[...] = jnp.sum(tmr[...].astype(F32), axis=0).astype(BF)
    loop(N_CTX - 1, t_start)
    pltpu.make_async_copy(th, tr.at[me], r_t.at[me]).start()

    def rs2_take(i):
        @pl.when(i != x)
        def _():
            arrived(rs2.at[i], r_rs2.at[i])
            own2[...] += rs2[i].astype(F32)

    def rs3_copy():
        return remote(rs3s, rs3, s_rs3, r_rs3, ctx=ypart)

    loop(4, rs2_take)
    rs3s[...] = own2[1 - yh].astype(BF)
    rs3_copy().start()
    backward_half(2)

    @pl.when(works)
    def _():
        for h in range(2):
            qm[h] = jnp.where((lane // 64) == h, qkv[0].astype(F32) * 0.125, 0.0).astype(BF)

        def keys(i):
            rows = pl.ds(mo(i * TILE, TILE), TILE)
            out = jnp.dot(ds[0, rows, :], qm[0], preferred_element_type=F32)
            out = out + jnp.dot(ds[1, rows, :], qm[1], preferred_element_type=F32)
            dbuf[1, rows, :] = out.astype(BF)
            p4_start(1, i)

        loop(FRAMES // TILE, keys)

    arrived(rs3, r_rs3)
    own3[0:96, :] = own2[yh] + rs3[...].astype(F32)
    ms[:, 0:32, :] = jnp.concatenate(
        [own3[...].T.reshape(N_DP, 24, 128), jnp.zeros((N_DP, 8, 128), F32)], axis=1
    ).astype(BF)
    dp_start()

    def p4_take(a):
        loop(TARGETS, lambda n: arrived(grad_r.at[a, n // PAIRS, n % PAIRS], r_p4.at[a * TARGETS + n]))

    for a, out in ((2, gv_ref), (0, gq_ref), (1, gk_ref)):
        p4_take(a)
        for u in range(2):
            for p in range(PAIRS):
                out[u, :, 128 * p:128 * p + 128] = grad_r[a, u, p]

    loop(N_CTX, lambda c: arrived(tr.at[c], r_t.at[c]))
    gt_ref[...] = jnp.sum(tr[...].astype(F32), axis=0)
    loop(N_DP, lambda d: arrived(mr.at[d], r_dp.at[d]))
    gw_ref[...] = jnp.sum(mr[...].astype(F32), axis=0)

    def sent(n):
        @pl.when(target_of(n) != me)
        def _():
            for a in range(3):
                p1_copy(a, n).wait_send()
            p3_copy(n).wait_send()

    loop(TARGETS, sent)

    def sent_dp(d):
        @pl.when(d != dp)
        def _():
            a_copy(d).wait_send()
            dp_copy(d).wait_send()
            td_copy(d).wait_send()

    loop(N_DP, sent_dp)

    def sent_ctx(c):
        @pl.when(c != me)
        def _():
            t_copy(c).wait_send()

            @pl.when(works)
            def _():
                p2_copy(c).wait_send()
                for a in range(3):
                    p4_copy(a, c).wait_send()

    loop(N_CTX, sent_ctx)
    w_y().wait_send()

    def sent_x(i):
        @pl.when(i != x)
        def _():
            w_x(i, 0).wait_send()
            w_x(i, 1).wait_send()
            rs2_copy(i).wait_send()

        rs1_copy(i).wait_send()

    loop(4, sent_x)
    loop(8, lambda i: w_sib(i).wait_send())
    rs3_copy().wait_send()
    for src, buf, base in ((hb, halo, 0), (gcb, ghalo, 12)):
        loop(col_tiles, lambda i: edges_do(src, buf, base, i, lambda copy: copy.wait_send()))


def finish(
    bo, gi, gq, gk, gv, gw_ref, gt_ref, bo_o, gi_o, gq_o, gk_o, gv_o, gw_o, gt_o,
    bo_v, gi_v, gq_v, gk_v, gv_v, gw_v, gt_v, in_sems, out_sems,
):
    held = (bo_v, gi_v, gq_v, gk_v, gv_v, gw_v, gt_v)
    outs = (bo_o, gi_o, gq_o, gk_o, gv_o, gw_o, gt_o)
    loads = [pltpu.make_async_copy(a, b, in_sems.at[i]) for i, (a, b) in enumerate(zip((bo, gi, gq, gk, gv), held))]
    stores = [pltpu.make_async_copy(a, b, out_sems.at[i]) for i, (a, b) in enumerate(zip(held, outs))]
    for load in loads:
        load.start()
    padded = jnp.concatenate([gw_ref[...], jnp.zeros((96, 128), F32)], axis=0).T
    gw_v[...] = padded[0:96, 0:24]
    stores[5].start()
    wide = jnp.concatenate([gt_ref[...], jnp.zeros((112, 128), F32)], axis=0).T
    gt_v[...] = jnp.concatenate([wide[32 * k:32 * k + TAPS, 0:16] for k in range(3)], axis=1)
    stores[6].start()
    for load, store in zip(loads, stores):
        load.wait()
        store.start()
    for store in stores:
        store.wait()


def per_device(frame_input, queries, key_proj, value_proj, out_weight, conv_weight, lengths, grad_output):
    right = jnp.pad(conv_weight.T, ((0, 0), (0, 1)))
    top = jnp.concatenate([out_weight.T, right[0:24]], axis=1)
    low = jnp.concatenate([right[24:32], right[32:40], right[40:48], jnp.zeros((8, 32), BF)], axis=1)
    message = jnp.concatenate([top, low], axis=0)
    vmem = pl.BlockSpec(memory_space=pltpu.VMEM)
    hbm = pl.BlockSpec(memory_space=pltpu.HBM)
    dma = lambda n: pltpu.SemaphoreType.DMA((n,))
    scratch = [
        ((2, ROWS, D), BF), ((2, ROWS, D), BF),
        ((3, FRAMES, 128), BF), ((2, FRAMES, 128), BF), ((2, FRAMES, 128), BF), ((128, FRAMES), BF),
        ((128, FRAMES), BF), ((2, FRAMES, FRAMES), BF), ((2, FRAMES, FRAMES), BF),
        ((FRAMES, 128), BF), ((2, PAIRS, ROWS, 128), BF), ((2 * ROWS, HD), BF), ((2, PAIRS, ROWS, 128), BF),
        ((FRAMES, 128), BF), ((3, FRAMES, 128), BF), ((3, 2, PAIRS, ROWS, 128), BF),
        ((N_DP, 32, 128), BF), ((32, D), F32), ((D, HD), BF),
        ((2, ROWS, D), F32), ((2, ROWS, D), BF), ((2, 2, 16, D), BF), ((2, 96, D), F32),
        ((2, ROWS, D), BF), ((2, 2, 16, D), BF), ((2, 96, D), F32), ((128, D), F32),
        ((8, 2, 96, HD), BF), ((8, 96, HD), BF), ((4, 2, 96, HD), BF), ((4, 2, 96, HD), BF),
        ((2, 96, HD), F32), ((96, HD), BF), ((96, HD), BF), ((128, HD), F32),
        ((N_DP, 32, 128), BF), ((N_DP, 32, 128), BF), ((N_DP, 16, 128), BF), ((N_DP, 16, 128), BF),
        ((16, 128), BF), ((N_CTX, 16, 128), BF),
    ]
    one = pltpu.SemaphoreType.DMA
    sems = [
        dma(2), dma(36), dma(48), dma(32), dma(32), dma(17), dma(16), dma(16), dma(12), dma(24), dma(24), dma(12),
        dma(16), dma(48), dma(36), dma(4), dma(4), dma(4), dma(4), one, one, dma(32), dma(32), dma(32), dma(32),
        dma(16), dma(16),
    ]
    shapes = (
        ((2, ROWS, D), BF), ((2, ROWS, D), BF), ((2, ROWS, HD), BF), ((2, ROWS, HD), BF), ((2, ROWS, HD), BF),
        ((32, 128), F32), ((16, 128), F32),
    )
    bo, gi, gq, gk, gv, gw, gt = pl.pallas_call(
        kernel,
        out_shape=[jax.ShapeDtypeStruct(s, t) for s, t in shapes],
        in_specs=[pl.BlockSpec(memory_space=pltpu.SMEM)] + [hbm] * 4 + [vmem, hbm],
        out_specs=[vmem] * 7,
        scratch_shapes=[pltpu.VMEM(s, t) for s, t in scratch] + sems,
        compiler_params=pltpu.CompilerParams(
            collective_id=0, has_side_effects=True, vmem_limit_bytes=60 * 1024 * 1024
        ),
        cost_estimate=pl.CostEstimate(flops=3 * 10**9, bytes_accessed=4 * 10**6, transcendentals=2 * 10**6),
    )(lengths, frame_input, queries, key_proj, value_proj, message, grad_output)
    final = shapes[0:5] + (((96, 24), F32), ((TAPS, 48), F32))
    return tuple(
        pl.pallas_call(
            finish,
            out_shape=[jax.ShapeDtypeStruct(s, t) for s, t in final],
            in_specs=[hbm] * 5 + [vmem] * 2,
            out_specs=[hbm] * 7,
            scratch_shapes=[pltpu.VMEM(s, t) for s, t in final] + [dma(5), dma(7)],
            compiler_params=pltpu.CompilerParams(vmem_limit_bytes=60 * 1024 * 1024),
            cost_estimate=pl.CostEstimate(flops=10**5, bytes_accessed=3 * 10**6, transcendentals=0),
        )(bo, gi, gq, gk, gv, gw, gt)
    )


def solution(mesh):
    rows = P("dp", "ctx", None)
    return jax.shard_map(
        per_device,
        mesh=mesh,
        in_specs=(rows, rows, rows, rows, P("ctx", "dp"), P(None, "dp"), P("dp"), rows),
        out_specs=(rows, rows, rows, rows, rows, P("ctx", "dp"), P(None, "dp")),
        check_vma=False,
    )
```

```python
import jax
import jax.numpy as jnp
from jax import lax
from jax.experimental import pallas as pl
from jax.experimental.pallas import tpu as pltpu
from jax.sharding import PartitionSpec as P

BF = jnp.bfloat16
F32 = jnp.float32
N_CTX = 16
N_DP = 32
ROWS = 64
FRAMES = 1024
D = 1536
HD = 768
PAIRS = 6
TARGETS = 2 * PAIRS
TAPS = 31
TILE = 256
CONV_BLOCKS = D // 128
NT = (((1,), (1,)), ((), ()))
TN = (((0,), (0,)), ((), ()))


def target_of(n):
    u, p = n // PAIRS, n % PAIRS
    hi = p // 4
    x = (1 - hi) * p + hi * (2 * (p - 4) + u)
    return 4 * x + 2 * u + hi


def remote(src, dst, send, recv, **axis):
    return pltpu.make_async_remote_copy(
        src_ref=src,
        dst_ref=dst,
        send_sem=send,
        recv_sem=recv,
        device_id=axis,
        device_id_type=pl.DeviceIdType.MESH,
    )


def arrived(dst, sem):
    pltpu.make_async_copy(dst, dst, sem).wait()


def loop(count, body):
    def step(i, carry):
        body(i)
        return carry

    lax.fori_loop(0, count, step, 0)


def mo(value, unit):
    return pl.multiple_of(value, unit)


def kernel(
    len_ref, x_ref, q_ref, k_ref, v_ref, wt_ref, cw_ref, go_ref,
    bo_ref, gi_ref, gq_ref, gk_ref, gv_ref, gw_ref, gt_ref,
    x_v, go_v, qkv, kx, qm, kt, vt, pt, ds, ob, att_r, att, ga_s, ga_r, dbuf, grad_r,
    w_a, taps, w_full, msg_ref,
    hid, hb, halo, hp, gcb, ghalo, gp, tgs,
    pp, rs1, rs2s, rs2, own2, rs3s, rs3, own3, ms, zr, ys, yr, tms, tzr, tys, tyr, th, tr,
    s_in, s_p1, r_p1, s_ay, r_ay, s_az, r_az, s_w, r_w, s_p2, r_p2, s_h, r_h, s_p3, r_p3, s_p4, r_p4,
    s_rs1, r_rs1, s_rs2, r_rs2, s_rs3, r_rs3, s_dp, r_dp, s_de, r_de, s_td, r_td, s_te, r_te, s_t, r_t,
):
    me = lax.axis_index("ctx")
    dp = lax.axis_index("dp")
    x = me // 4
    yh = (me // 2) % 2
    core = me % 2
    sib = 4 * x + 2 * yh + (1 - core)
    ypart = 4 * x + 2 * (1 - yh) + core
    pair = (1 - core) * x + core * (4 + x // 2)
    works = (core * ((x + yh) % 2)) == 0
    zi, yl = dp // 4, dp % 4
    my_rows = pl.ds(mo(me * ROWS, ROWS), ROWS)
    inputs = (q_ref, k_ref, v_ref)

    loads = [pltpu.make_async_copy(a, b, s_in.at[i]) for i, (a, b) in enumerate(((x_ref, x_v), (go_ref, go_v)))]
    for load in loads:
        load.start()

    wide = jnp.concatenate([cw_ref[...].astype(F32), jnp.zeros((TAPS, 80), F32)], axis=1)
    right = jnp.concatenate([wide, jnp.zeros((128 - TAPS, 128), F32)], axis=0).T[0:48, 0:32]
    top = jnp.concatenate([wt_ref[...].astype(F32), right[0:24]], axis=1)
    low = jnp.concatenate([right[24:32], right[32:40], right[40:48], jnp.zeros((8, 32), F32)], axis=1)
    msg_ref[...] = jnp.concatenate([top, low], axis=0).astype(BF)

    barrier = pltpu.get_barrier_semaphore()

    def greet_ctx(i):
        @pl.when(i != me)
        def _():
            pl.semaphore_signal(barrier, inc=1, device_id={"ctx": i}, device_id_type=pl.DeviceIdType.MESH)

    def z_peer(i):
        return 4 * lax.rem(zi + 1 + i, 8) + yl

    def y_peer(i):
        return 4 * zi + lax.rem(yl + 1 + i, 4)

    def greet_dp(to):
        pl.semaphore_signal(barrier, inc=1, device_id={"dp": to}, device_id_type=pl.DeviceIdType.MESH)

    loop(N_CTX, greet_ctx)
    loop(7, lambda i: greet_dp(z_peer(i)))
    loop(3, lambda i: greet_dp(y_peer(i)))
    pl.semaphore_wait(barrier, N_CTX - 1 + 7 + 3)

    def p1_parts(a, n):
        src = inputs[a].at[n // PAIRS, :, pl.ds(mo((n % PAIRS) * 128, 128), 128)]
        return src, qkv.at[a, my_rows, :]

    def p1_copy(a, n):
        src, dst = p1_parts(a, n)
        return remote(src, dst, s_p1, r_p1.at[a], ctx=target_of(n))

    def p1_start(a):
        def one(i):
            n = lax.rem(i + me, TARGETS)
            t = target_of(n)

            @pl.when(t != me)
            def _():
                p1_copy(a, n).start()

            @pl.when(t == me)
            def _():
                src, dst = p1_parts(a, n)
                pltpu.make_async_copy(src, dst, r_p1.at[a]).start()

        loop(TARGETS, one)

    four = pl.ds(4 * zi, 4)

    def a_y(i):
        remote(msg_ref, w_a.at[dp], s_ay, r_ay, dp=y_peer(i)).start()

    def a_z(i):
        remote(w_a.at[four], w_a.at[four], s_az, r_az.at[zi], dp=z_peer(i)).start()

    def a_z_take(i):
        source = lax.rem(zi + 1 + i, 8)
        arrived(w_a.at[pl.ds(4 * source, 4)], r_az.at[source])

    loop(3, a_y)
    pltpu.make_async_copy(msg_ref, w_a.at[dp], r_ay).start()
    p1_start(1)
    arrived(w_a.at[four], r_ay)
    loop(7, a_z)
    p1_start(0)
    p1_start(2)
    tgs[...] = jnp.zeros_like(tgs)
    own3[...] = jnp.zeros_like(own3)
    loop(7, a_z_take)
    pieces = w_a[...].astype(F32)
    block = pieces[:, 0:24, :].reshape(HD, 128).T
    rest = pieces[:, 24:32, :].reshape(N_DP * 8, 128)
    moved_rest = [pltpu.roll(rest, 96 - 32 * k, 1).reshape(N_DP, 8, 128) for k in range(3)]
    taps[...] = jnp.concatenate([pieces[:, 0:24, :]] + moved_rest, axis=1).reshape(D, 128).T[96:128, :]

    def w_rows(c):
        return w_full.at[pl.ds(mo(c * 96, 32), 96), :]

    w_full[pl.ds(mo(me * 96, 32), 96), :] = block[0:96, :].astype(BF)

    def w_copy(c, slot, to):
        return remote(w_rows(c), w_rows(c), s_w.at[slot], r_w.at[c], ctx=to)

    def w_y():
        return w_copy(me, 0, ypart)

    def w_x(i, y):
        return w_copy(4 * x + 2 * y + core, 1 + 4 * y + i, 4 * i + 2 * yh + core)

    def w_sib(i):
        return w_copy(2 * i + core, 9 + i, sib)

    w_y().start()

    def w_x_start(y):
        def one(i):
            @pl.when(i != x)
            def _():
                w_x(i, y).start()

        loop(4, one)

    w_x_start(yh)

    lane = lax.broadcasted_iota(jnp.int32, (FRAMES, 128), 1)

    def p1_take(a):
        arrived(qkv.at[a], r_p1.at[a])

    @pl.when(works)
    def _():
        p1_take(1)
        row = lax.broadcasted_iota(jnp.int32, (FRAMES, 128), 0)
        bias = jnp.where(row < len_ref[yh], 0.0, -1e30)
        k = qkv[1].astype(F32)
        for h in range(2):
            kx[h] = jnp.where(lane == 64 * (1 - h), bias, k).astype(BF)
        kt[...] = k.T.astype(BF)
        p1_take(0)
        q = qkv[0].astype(F32) * 0.125
        for h in range(2):
            mine = (lane // 64) == h
            qm[h] = jnp.where(mine, q, jnp.where(lane == 64 * (1 - h), 1.0, 0.0)).astype(BF)

    def weights_of(h):
        @pl.when(works)
        def _():
            def tile(i):
                cols = pl.ds(mo(i * TILE, TILE), TILE)
                s = lax.dot_general(kx[h], qm[h, cols, :], NT, preferred_element_type=F32)
                e = jnp.exp(s - jnp.max(s, axis=0, keepdims=True))
                pt[h, :, cols] = (e * (1.0 / jnp.sum(e, axis=0, keepdims=True))).astype(BF)

            loop(FRAMES // TILE, tile)

    weights_of(0)
    arrived(w_rows(ypart), r_w.at[ypart])
    w_x_start(1 - yh)
    weights_of(1)

    def p2_copy(c):
        rows = pl.ds(mo(c * ROWS, ROWS), ROWS)
        return remote(ob.at[rows, :], att_r.at[yh, pair], s_p2, r_p2, ctx=c)

    def p2_start(c):
        @pl.when(c != me)
        def _():
            p2_copy(c).start()

        @pl.when(c == me)
        def _():
            pltpu.make_async_copy(ob.at[my_rows, :], att_r.at[yh, pair], r_p2).start()

    @pl.when(works)
    def _():
        p1_take(2)
        vt[...] = qkv[2].astype(F32).T.astype(BF)

        def tile(i):
            cols = pl.ds(mo(i * TILE, TILE), TILE)
            out = [
                jnp.dot(vt[64 * h:64 * h + 64, :], pt[h, :, cols], preferred_element_type=F32) for h in range(2)
            ]
            ob[cols, :] = jnp.concatenate(out, axis=0).T.astype(BF)
            loop(TILE // ROWS, lambda j: p2_start(i * (TILE // ROWS) + j))

        loop(FRAMES // TILE, tile)

    def w_forward(i):
        c = 2 * i + core

        @pl.when(((c - me) * (c - ypart)) != 0)
        def _():
            arrived(w_rows(c), r_w.at[c])

        w_sib(i).start()

    loop(8, w_forward)

    def w_last(i):
        c = 2 * i + (1 - core)
        arrived(w_rows(c), r_w.at[c])

    loop(8, w_last)
    arrived(att_r, r_p2)
    for u in range(2):
        for p in range(PAIRS):
            att[64 * u:64 * u + 64, 128 * p:128 * p + 128] = att_r[u, p]

    frame = lax.broadcasted_iota(jnp.int32, (ROWS, TILE), 0) + me * ROWS
    before, after = me > 0, me < N_CTX - 1
    col_tiles = D // TILE

    def edge_copies(src, buf, base, i):
        cols = pl.ds(mo(i * TILE, TILE), TILE)
        up = remote(
            src.at[:, 48:64, cols], buf.at[0, :, :, cols], s_h.at[base + i], r_h.at[base + i],
            ctx=lax.rem(me + 1, N_CTX),
        )
        down = remote(
            src.at[:, 0:16, cols], buf.at[1, :, :, cols], s_h.at[base + 6 + i], r_h.at[base + 6 + i],
            ctx=lax.rem(me + N_CTX - 1, N_CTX),
        )
        return up, down

    def edges_do(src, buf, base, i, what):
        up, down = edge_copies(src, buf, base, i)

        @pl.when(after)
        def _():
            what(up)

        @pl.when(before)
        def _():
            what(down)

    def edges_take(buf, base, padded, i):
        cols = pl.ds(mo(i * TILE, TILE), TILE)
        for side, first, inner in ((0, 0, before), (1, 80, after)):
            @pl.when(inner)
            def _():
                arrived(buf.at[side, :, :, cols], r_h.at[base + 6 * side + i])
                padded[:, first:first + 16, cols] = buf[side, :, :, cols].astype(F32)

            @pl.when(jnp.logical_not(inner))
            def _():
                padded[:, first:first + 16, cols] = jnp.zeros((2, 16, TILE), F32)

    def rolled_by(block, r):
        return block if r == 0 else pltpu.roll(block, 96 - r, 0)

    for load in loads:
        load.wait()

    def project(i):
        cols = pl.ds(mo(i * TILE, TILE), TILE)
        out = lax.dot_general(att[...], w_full[cols, :], NT, preferred_element_type=F32)
        for u in range(2):
            h = (out[64 * u:64 * u + 64, :] + x_v[u, :, cols].astype(F32)).astype(BF).astype(F32)
            masked = jnp.where(frame < len_ref[u], h, 0.0)
            hid[u, :, cols] = h
            hb[u, :, cols] = masked.astype(BF)
            hp[u, 16:80, cols] = masked
        edges_do(hb, halo, 0, i, lambda copy: copy.start())

    loop(col_tiles, project)

    def conv_forward(i):
        edges_take(halo, 0, hp, i)
        for half in range(2):
            cols = pl.ds(mo(i * TILE + half * 128, 128), 128)
            w = taps[:, cols]
            for u in range(2):
                block = hp[u, :, cols]
                acc = jnp.zeros((ROWS, 128), F32)
                for r in range(8):
                    moved = rolled_by(block, r)
                    for a in range(4):
                        j = 8 * a + r - 1
                        if 0 <= j < TAPS:
                            acc = acc + w[j:j + 1, :] * moved[8 * a:8 * a + ROWS, :]
                sg = jax.nn.sigmoid(acc)
                bo_ref[u, :, cols] = (hid[u, :, cols] + acc * sg).astype(BF)
                gc = (go_v[u, :, cols].astype(F32) * (sg * (1.0 + acc * (1.0 - sg)))).astype(BF)
                gcb[u, :, cols] = gc
                gp[u, 16:80, cols] = gc.astype(F32)
        edges_do(gcb, ghalo, 12, i, lambda copy: copy.start())

    loop(col_tiles, conv_forward)

    def taps_gradient(i):
        cols = pl.ds(mo(i * 128, 128), 128)
        blocks = [hp[u, :, cols] for u in range(2)]
        grads = [gp[u, 16:80, cols] for u in range(2)]
        for r in range(8):
            moved = [rolled_by(block, r) for block in blocks]
            for a in range(4):
                j = 8 * a + r - 1
                if 0 <= j < TAPS:
                    total = sum(g * m[8 * a:8 * a + ROWS, :] for g, m in zip(grads, moved))
                    tgs[j:j + 1, cols] = jnp.sum(total, axis=0, keepdims=True)

    loop(CONV_BLOCKS, taps_gradient)
    frame_c = lax.broadcasted_iota(jnp.int32, (ROWS, 128), 0) + me * ROWS

    def conv_backward(i):
        edges_take(ghalo, 12, gp, i)
        for half in range(2):
            cols = pl.ds(mo(i * TILE + half * 128, 128), 128)
            w = taps[:, cols]
            for u in range(2):
                block = gp[u, :, cols]
                acc = jnp.zeros((ROWS, 128), F32)
                for r in range(8):
                    moved = rolled_by(block, r)
                    for a in range(4):
                        j = 31 - (8 * a + r)
                        if 0 <= j < TAPS:
                            acc = acc + w[j:j + 1, :] * moved[8 * a:8 * a + ROWS, :]
                gi = go_v[u, :, cols].astype(F32) + jnp.where(frame_c < len_ref[u], acc, 0.0)
                gi_ref[u, :, cols] = gi.astype(BF)

    loop(col_tiles, conv_backward)

    def p3_copy(n):
        return remote(
            ga_s.at[n // PAIRS, n % PAIRS], ga_r.at[my_rows, :], s_p3, r_p3, ctx=target_of(n)
        )

    gi_rows = gi_ref[...].reshape(2 * ROWS, D)

    def p3_start(n):
        t = target_of(n)

        @pl.when(t != me)
        def _():
            p3_copy(n).start()

        @pl.when(t == me)
        def _():
            pltpu.make_async_copy(ga_s.at[n // PAIRS, n % PAIRS], ga_r.at[my_rows, :], r_p3).start()

    def cotangent(i):
        cols = pl.ds(mo(i * TILE, TILE), TILE)
        out = jnp.dot(gi_rows, w_full[:, cols], preferred_element_type=F32).astype(BF)
        for u in range(2):
            for half in range(2):
                ga_s[u, 2 * i + half] = out[64 * u:64 * u + 64, 128 * half:128 * half + 128]
        loop(4, lambda m: p3_start((m // 2) * PAIRS + 2 * i + m % 2))

    loop(HD // TILE, cotangent)

    tap_rows = tgs[...].T.reshape(N_DP, 48, 128)
    packed = [tap_rows[:, 0:16, :]] + [
        pltpu.roll(tap_rows[:, 16 * k:16 * k + 16, :].reshape(N_DP * 16, 128), 32 * k, 1).reshape(N_DP, 16, 128)
        for k in (1, 2)
    ]
    tms[...] = (packed[0] + packed[1] + packed[2]).astype(BF)

    def over_dp(src, zr, ys, yr, s_z, r_z, s_y, r_y):
        def first(i):
            to = z_peer(i)
            remote(src.at[pl.ds(to - yl, 4)], zr.at[zi], s_z, r_z, dp=to).start()

        def start():
            loop(7, first)
            pltpu.make_async_copy(src.at[four], zr.at[zi], r_z).start()

        def second(i):
            to = y_peer(i)
            remote(ys.at[to - 4 * zi], yr.at[yl], s_y, r_y, dp=to).start()

        def turn():
            arrived(zr, r_z)
            ys[...] = jnp.sum(zr[...].astype(F32), axis=0).astype(BF)
            loop(3, second)
            pltpu.make_async_copy(ys.at[yl], yr.at[yl], r_y).start()

        def end():
            arrived(yr, r_y)
            return jnp.sum(yr[...].astype(F32), axis=0)

        def sent():
            arrived(src.at[0:28], s_z)
            arrived(ys.at[0:3], s_y)

        return start, turn, end, sent

    td_start, td_turn, td_end, td_sent = over_dp(tms, tzr, tys, tyr, s_td, r_td, s_te, r_te)
    dp_start, dp_turn, dp_end, dp_sent = over_dp(ms, zr, ys, yr, s_dp, r_dp, s_de, r_de)

    def rs1_copy(i):
        return remote(
            pp.at[pl.ds(2 * i, 2), 1 - core], rs1.at[pl.ds(2 * i, 2)], s_rs1.at[i], r_rs1.at[i], ctx=sib
        )

    def panel(i):
        cols = pl.ds(mo(i * 384, 128), 384)
        gi_cols = jnp.concatenate([gi_ref[0, :, cols], gi_ref[1, :, cols]], axis=0)
        out = lax.dot_general(gi_cols, att[...], TN, preferred_element_type=F32)
        pp[pl.ds(2 * i, 2)] = out.reshape(2, 2, 96, HD).astype(BF)
        rs1_copy(i).start()

    loop(4, panel)
    td_start()

    def rs2_copy(i):
        return remote(rs2s.at[i], rs2.at[x], s_rs2.at[i], r_rs2.at[x], ctx=4 * i + 2 * yh + core)

    def rs2_start(i):
        two = pl.ds(2 * i, 2)
        arrived(rs1.at[two], r_rs1.at[i])
        total = pp[two, core].astype(F32) + rs1[two].astype(F32)

        @pl.when(i != x)
        def _():
            rs2s[i] = total.astype(BF)
            rs2_copy(i).start()

        @pl.when(i == x)
        def _():
            own2[...] = total

    loop(4, rs2_start)

    def p4_copy(a, c):
        rows = pl.ds(mo(c * ROWS, ROWS), ROWS)
        return remote(
            dbuf.at[a, rows, :], grad_r.at[a, yh, pair], s_p4, r_p4.at[a], ctx=c,
        )

    def p4_start(a, i):
        def one(j):
            c = i * (TILE // ROWS) + j

            @pl.when(c != me)
            def _():
                p4_copy(a, c).start()

            @pl.when(c == me)
            def _():
                pltpu.make_async_copy(dbuf.at[a, my_rows, :], grad_r.at[a, yh, pair], r_p4.at[a]).start()

        loop(TILE // ROWS, one)

    tile_lane = lax.broadcasted_iota(jnp.int32, (TILE, 128), 1) // 64

    @pl.when(works)
    def _():
        arrived(ga_r, r_p3)

        def values(i):
            rows = pl.ds(mo(i * TILE, TILE), TILE)
            first = jnp.dot(pt[0, rows, :], ga_r[...], preferred_element_type=F32)
            second = jnp.dot(pt[1, rows, :], ga_r[...], preferred_element_type=F32)
            dbuf[2, rows, :] = jnp.where(tile_lane == 0, first, second).astype(BF)
            p4_start(2, i)

        loop(FRAMES // TILE, values)

    def backward_tile(i):
        cols = pl.ds(mo(i * TILE, TILE), TILE)
        ga = ga_r[cols, :].astype(F32)
        prod = (ga * ob[cols, :].astype(F32)).T
        parts = []
        for h in range(2):
            gmb = jnp.where(tile_lane == h, ga, 0.0).astype(BF)
            delta = jnp.sum(prod[64 * h:64 * h + 64, :], axis=0, keepdims=True)
            dpt = lax.dot_general(qkv[2], gmb, NT, preferred_element_type=F32)
            dst = (pt[h, :, cols].astype(F32) * (dpt - delta)).astype(BF)
            ds[h, :, cols] = dst
            parts.append(jnp.dot(kt[64 * h:64 * h + 64, :], dst, preferred_element_type=F32))
        dbuf[0, cols, :] = (jnp.concatenate(parts, axis=0).T * 0.125).astype(BF)
        p4_start(0, i)

    def backward_half(first):
        @pl.when(works)
        def _():
            loop(2, lambda i: backward_tile(i + first))

    td_turn()

    def rs2_take(i):
        @pl.when(i != x)
        def _():
            arrived(rs2.at[i], r_rs2.at[i])
            own2[...] += rs2[i].astype(F32)

    def rs3_copy():
        return remote(rs3s, rs3, s_rs3, r_rs3, ctx=ypart)

    loop(4, rs2_take)
    rs3s[...] = own2[1 - yh].astype(BF)
    rs3_copy().start()
    backward_half(0)

    def t_copy(c):
        return remote(th, tr.at[me], s_t, r_t, ctx=c)

    def t_start(i):
        t_copy(lax.rem(i + 1 + me, N_CTX)).start()

    th[...] = td_end().astype(BF)
    loop(N_CTX - 1, t_start)
    pltpu.make_async_copy(th, tr.at[me], r_t).start()
    arrived(rs3, r_rs3)
    own3[0:96, :] = own2[yh] + rs3[...].astype(F32)
    ms[...] = jnp.concatenate(
        [own3[...].T.reshape(N_DP, 24, 128), jnp.zeros((N_DP, 8, 128), F32)], axis=1
    ).astype(BF)
    dp_start()
    backward_half(2)

    @pl.when(works)
    def _():
        for h in range(2):
            qm[h] = jnp.where((lane // 64) == h, qkv[0].astype(F32) * 0.125, 0.0).astype(BF)

        def keys(i):
            rows = pl.ds(mo(i * TILE, TILE), TILE)
            out = jnp.dot(ds[0, rows, :], qm[0], preferred_element_type=F32)
            out = out + jnp.dot(ds[1, rows, :], qm[1], preferred_element_type=F32)
            dbuf[1, rows, :] = out.astype(BF)
            p4_start(1, i)

        loop(FRAMES // TILE, keys)

    dp_turn()

    def p4_take(a):
        arrived(grad_r.at[a], r_p4.at[a])

    for a, out in ((2, gv_ref), (0, gq_ref), (1, gk_ref)):
        p4_take(a)
        for u in range(2):
            for p in range(PAIRS):
                out[u, :, 128 * p:128 * p + 128] = grad_r[a, u, p]

    arrived(tr, r_t)
    gt_ref[...] = jnp.sum(tr[...].astype(F32), axis=0)
    gw_ref[...] = dp_end()

    arrived(w_a.at[0:3], s_ay)
    arrived(w_a.at[0:28], s_az)
    td_sent()
    dp_sent()
    arrived(tr.at[0:N_CTX - 1], s_t)
    others = ROWS * (N_CTX - 1)

    @pl.when(works)
    def _():
        arrived(qkv.at[:, 0:ROWS * (TARGETS - 1), :], s_p1)
        arrived(ga_r.at[0:ROWS * (TARGETS - 1), :], s_p3)
        arrived(ob.at[0:others, :], s_p2)
        arrived(dbuf.at[:, 0:others, :], s_p4)

    @pl.when(jnp.logical_not(works))
    def _():
        arrived(qkv.at[:, 0:ROWS * TARGETS, :], s_p1)
        arrived(ga_r.at[0:ROWS * TARGETS, :], s_p3)

    w_y().wait_send()

    def sent_x(i):
        @pl.when(i != x)
        def _():
            w_x(i, 0).wait_send()
            w_x(i, 1).wait_send()
            rs2_copy(i).wait_send()

        rs1_copy(i).wait_send()

    loop(4, sent_x)
    loop(8, lambda i: w_sib(i).wait_send())
    rs3_copy().wait_send()
    for src, buf, base in ((hb, halo, 0), (gcb, ghalo, 12)):
        loop(col_tiles, lambda i: edges_do(src, buf, base, i, lambda copy: copy.wait_send()))


def finish(
    bo, gi, gq, gk, gv, gw_ref, gt_ref, bo_o, gi_o, gq_o, gk_o, gv_o, gw_o, gt_o,
    bo_v, gi_v, gq_v, gk_v, gv_v, gw_v, gt_v, in_sems, out_sems,
):
    held = (bo_v, gi_v, gq_v, gk_v, gv_v, gw_v, gt_v)
    outs = (bo_o, gi_o, gq_o, gk_o, gv_o, gw_o, gt_o)
    loads = [pltpu.make_async_copy(a, b, in_sems.at[i]) for i, (a, b) in enumerate(zip((bo, gi, gq, gk, gv), held))]
    stores = [pltpu.make_async_copy(a, b, out_sems.at[i]) for i, (a, b) in enumerate(zip(held, outs))]
    for load in loads:
        load.start()
    gw_v[...] = gw_ref[0:24, 0:96]
    stores[5].start()
    wide = jnp.concatenate([gt_ref[...], jnp.zeros((112, 128), F32)], axis=0).T
    gt_v[...] = jnp.concatenate([wide[32 * k:32 * k + TAPS, 0:16] for k in range(3)], axis=1)
    stores[6].start()
    for load, store in zip(loads, stores):
        load.wait()
        store.start()
    for store in stores:
        store.wait()


def per_device(frame_input, queries, key_proj, value_proj, out_weight, conv_weight, lengths, grad_output):
    vmem = pl.BlockSpec(memory_space=pltpu.VMEM)
    hbm = pl.BlockSpec(memory_space=pltpu.HBM)
    dma = lambda n: pltpu.SemaphoreType.DMA((n,))
    scratch = [
        ((2, ROWS, D), BF), ((2, ROWS, D), BF),
        ((3, FRAMES, 128), BF), ((2, FRAMES, 128), BF), ((2, FRAMES, 128), BF), ((128, FRAMES), BF),
        ((128, FRAMES), BF), ((2, FRAMES, FRAMES), BF), ((2, FRAMES, FRAMES), BF),
        ((FRAMES, 128), BF), ((2, PAIRS, ROWS, 128), BF), ((2 * ROWS, HD), BF), ((2, PAIRS, ROWS, 128), BF),
        ((FRAMES, 128), BF), ((3, FRAMES, 128), BF), ((3, 2, PAIRS, ROWS, 128), BF),
        ((N_DP, 32, 128), BF), ((32, D), F32), ((D, HD), BF), ((32, 128), BF),
        ((2, ROWS, D), F32), ((2, ROWS, D), BF), ((2, 2, 16, D), BF), ((2, 96, D), F32),
        ((2, ROWS, D), BF), ((2, 2, 16, D), BF), ((2, 96, D), F32), ((128, D), F32),
        ((8, 2, 96, HD), BF), ((8, 96, HD), BF), ((4, 2, 96, HD), BF), ((4, 2, 96, HD), BF),
        ((2, 96, HD), F32), ((96, HD), BF), ((96, HD), BF), ((128, HD), F32),
        ((N_DP, 32, 128), BF), ((8, 4, 32, 128), BF), ((4, 32, 128), BF), ((4, 32, 128), BF),
        ((N_DP, 16, 128), BF), ((8, 4, 16, 128), BF), ((4, 16, 128), BF), ((4, 16, 128), BF),
        ((16, 128), BF), ((N_CTX, 16, 128), BF),
    ]
    one = pltpu.SemaphoreType.DMA
    sems = [
        dma(2), one, dma(3), one, one, one, dma(8), dma(17), dma(16), one, one, dma(24), dma(24), one, one, one,
        dma(3), dma(4), dma(4), dma(4), dma(4), one, one, one, one, one, one, one, one, one, one, one, one,
    ]
    shapes = (
        ((2, ROWS, D), BF), ((2, ROWS, D), BF), ((2, ROWS, HD), BF), ((2, ROWS, HD), BF), ((2, ROWS, HD), BF),
        ((32, 128), F32), ((16, 128), F32),
    )
    bo, gi, gq, gk, gv, gw, gt = pl.pallas_call(
        kernel,
        out_shape=[jax.ShapeDtypeStruct(s, t) for s, t in shapes],
        in_specs=[pl.BlockSpec(memory_space=pltpu.SMEM)] + [hbm] * 4 + [vmem, vmem, hbm],
        out_specs=[vmem] * 7,
        scratch_shapes=[pltpu.VMEM(s, t) for s, t in scratch] + sems,
        compiler_params=pltpu.CompilerParams(
            collective_id=0, has_side_effects=True, vmem_limit_bytes=60 * 1024 * 1024
        ),
        cost_estimate=pl.CostEstimate(flops=3 * 10**9, bytes_accessed=4 * 10**6, transcendentals=2 * 10**6),
    )(lengths, frame_input, queries, key_proj, value_proj, out_weight.T, conv_weight, grad_output)
    final = shapes[0:5] + (((24, 96), F32), ((TAPS, 48), F32))
    bo, gi, gq, gk, gv, gw, gt = (
        pl.pallas_call(
            finish,
            out_shape=[jax.ShapeDtypeStruct(s, t) for s, t in final],
            in_specs=[hbm] * 5 + [vmem] * 2,
            out_specs=[hbm] * 7,
            scratch_shapes=[pltpu.VMEM(s, t) for s, t in final] + [dma(5), dma(7)],
            compiler_params=pltpu.CompilerParams(vmem_limit_bytes=60 * 1024 * 1024),
            cost_estimate=pl.CostEstimate(flops=10**5, bytes_accessed=3 * 10**6, transcendentals=0),
        )(bo, gi, gq, gk, gv, gw, gt)
    )
    return bo, gi, gq, gk, gv, gw.T, gt


def solution(mesh):
    rows = P("dp", "ctx", None)
    return jax.shard_map(
        per_device,
        mesh=mesh,
        in_specs=(rows, rows, rows, rows, P("ctx", "dp"), P(None, "dp"), P("dp"), rows),
        out_specs=(rows, rows, rows, rows, rows, P("ctx", "dp"), P(None, "dp")),
        check_vma=False,
    )
```

```python
import jax
import jax.numpy as jnp
from jax import lax
from jax.experimental import pallas as pl
from jax.experimental.pallas import tpu as pltpu
from jax.sharding import PartitionSpec as P

BF = jnp.bfloat16
F32 = jnp.float32
N_CTX = 16
N_DP = 32
ROWS = 64
FRAMES = 1024
D = 1536
HD = 768
PAIRS = 6
TARGETS = 2 * PAIRS
TAPS = 31
TILE = 256
CONV_BLOCKS = D // 128
NT = (((1,), (1,)), ((), ()))
TN = (((0,), (0,)), ((), ()))


def target_of(n):
    u, p = n // PAIRS, n % PAIRS
    hi = p // 4
    x = (1 - hi) * p + hi * (2 * (p - 4) + u)
    return 4 * x + 2 * u + hi


def remote(src, dst, send, recv, **axis):
    return pltpu.make_async_remote_copy(
        src_ref=src,
        dst_ref=dst,
        send_sem=send,
        recv_sem=recv,
        device_id=axis,
        device_id_type=pl.DeviceIdType.MESH,
    )


def arrived(dst, sem):
    pltpu.make_async_copy(dst, dst, sem).wait()


def loop(count, body):
    def step(i, carry):
        body(i)
        return carry

    lax.fori_loop(0, count, step, 0)


def mo(value, unit):
    return pl.multiple_of(value, unit)


def kernel(
    len_ref, x_ref, q_ref, k_ref, v_ref, wt_ref, cw_ref, go_ref,
    bo_ref, gi_ref, gq_ref, gk_ref, gv_ref, gw_ref, gt_ref,
    x_v, go_v, qkv, kx, qm, kt, vt, pt, ds, ob, att_r, att, ga_s, ga_r, dbuf, grad_r,
    w_a, taps, w_full, msg_ref,
    hid, hb, halo, hp, gcb, ghalo, gp, tgs,
    pp, rs1, rs2s, rs2, own2, own3, ms, zr, ys, yr, tms, tzr, tys, tyr, th, tr,
    s_in, s_p1, r_p1, s_ay, r_ay, s_az, r_az, s_w, r_w, s_p2, r_p2, s_h, r_h, s_p3, r_p3, s_p4, r_p4,
    s_rs1, r_rs1, s_rs2, r_rs2, s_dp, r_dp, s_de, r_de, s_td, r_td, s_te, r_te, s_t, r_t,
):
    me = lax.axis_index("ctx")
    dp = lax.axis_index("dp")
    x = me // 4
    yh = (me // 2) % 2
    core = me % 2
    sib = 4 * x + 2 * yh + (1 - core)
    ypart = 4 * x + 2 * (1 - yh) + core
    pair = (1 - core) * x + core * (4 + x // 2)
    works = (core * ((x + yh) % 2)) == 0
    zi, yl = dp // 4, dp % 4
    my_rows = pl.ds(mo(me * ROWS, ROWS), ROWS)
    inputs = (q_ref, k_ref, v_ref)

    loads = [pltpu.make_async_copy(a, b, s_in.at[i]) for i, (a, b) in enumerate(((x_ref, x_v), (go_ref, go_v)))]
    for load in loads:
        load.start()

    wide = jnp.concatenate([cw_ref[...].astype(F32), jnp.zeros((TAPS, 80), F32)], axis=1)
    right = jnp.concatenate([wide, jnp.zeros((128 - TAPS, 128), F32)], axis=0).T[0:48, 0:32]
    top = jnp.concatenate([wt_ref[...].astype(F32), right[0:24]], axis=1)
    low = jnp.concatenate([right[24:32], right[32:40], right[40:48], jnp.zeros((8, 32), F32)], axis=1)
    msg_ref[...] = jnp.concatenate([top, low], axis=0).astype(BF)

    barrier = pltpu.get_barrier_semaphore()

    def greet_ctx(i):
        @pl.when(i != me)
        def _():
            pl.semaphore_signal(barrier, inc=1, device_id={"ctx": i}, device_id_type=pl.DeviceIdType.MESH)

    def z_peer(i):
        return 4 * lax.rem(zi + 1 + i, 8) + yl

    def y_peer(i):
        return 4 * zi + lax.rem(yl + 1 + i, 4)

    def ring_peer(i):
        o = lax.rem(4 * yh + yl + 1 + i, 8)
        return o // 4, o % 4, {"ctx": 4 * x + 2 * (o // 4) + core, "dp": 4 * zi + o % 4}

    def greet(to):
        pl.semaphore_signal(barrier, inc=1, device_id=to, device_id_type=pl.DeviceIdType.MESH)

    loop(N_CTX, greet_ctx)
    loop(7, lambda i: greet({"dp": z_peer(i)}))
    loop(7, lambda i: greet(ring_peer(i)[2]))
    pl.semaphore_wait(barrier, N_CTX - 1 + 7 + 7)

    def p1_parts(a, n):
        src = inputs[a].at[n // PAIRS, :, pl.ds(mo((n % PAIRS) * 128, 128), 128)]
        return src, qkv.at[a, my_rows, :]

    def p1_copy(a, n):
        src, dst = p1_parts(a, n)
        return remote(src, dst, s_p1, r_p1.at[a], ctx=target_of(n))

    def p1_start(a):
        def one(i):
            n = lax.rem(i + me, TARGETS)
            t = target_of(n)

            @pl.when(t != me)
            def _():
                p1_copy(a, n).start()

            @pl.when(t == me)
            def _():
                src, dst = p1_parts(a, n)
                pltpu.make_async_copy(src, dst, r_p1.at[a]).start()

        loop(TARGETS, one)

    four = pl.ds(4 * zi, 4)

    def a_y(i):
        remote(msg_ref, w_a.at[yh, dp], s_ay, r_ay, **ring_peer(i)[2]).start()

    def a_z(i):
        remote(w_a.at[:, four], w_a.at[:, four], s_az, r_az.at[zi], dp=z_peer(i)).start()

    def a_z_take(i):
        source = lax.rem(zi + 1 + i, 8)
        arrived(w_a.at[:, pl.ds(4 * source, 4)], r_az.at[source])

    loop(7, a_y)
    pltpu.make_async_copy(msg_ref, w_a.at[yh, dp], r_ay).start()
    p1_start(1)
    arrived(w_a.at[:, four], r_ay)
    loop(7, a_z)
    p1_start(0)
    p1_start(2)
    tgs[...] = jnp.zeros_like(tgs)
    own3[...] = jnp.zeros_like(own3)
    loop(7, a_z_take)
    for y in range(2):
        pieces = w_a[y].astype(F32)
        block = pieces[:, 0:24, :].reshape(HD, 128).T
        w_full[pl.ds(mo((4 * x + 2 * y + core) * 96, 32), 96), :] = block[0:96, :].astype(BF)
        if y == 0:
            rest = pieces[:, 24:32, :].reshape(N_DP * 8, 128)
            moved_rest = [pltpu.roll(rest, 96 - 32 * k, 1).reshape(N_DP, 8, 128) for k in range(3)]
            taps[...] = jnp.concatenate([pieces[:, 0:24, :]] + moved_rest, axis=1).reshape(D, 128).T[96:128, :]

    def w_rows(c):
        return w_full.at[pl.ds(mo(c * 96, 32), 96), :]

    def w_copy(c, slot, to):
        return remote(w_rows(c), w_rows(c), s_w.at[slot], r_w.at[c], ctx=to)

    def w_x(i, y):
        return w_copy(4 * x + 2 * y + core, 1 + 4 * y + i, 4 * i + 2 * yh + core)

    def w_sib(i):
        return w_copy(2 * i + core, 9 + i, sib)

    def w_x_start(y):
        def one(i):
            @pl.when(i != x)
            def _():
                w_x(i, y).start()

        loop(4, one)

    w_x_start(0)
    w_x_start(1)

    lane = lax.broadcasted_iota(jnp.int32, (FRAMES, 128), 1)

    def p1_take(a):
        arrived(qkv.at[a], r_p1.at[a])

    @pl.when(works)
    def _():
        p1_take(1)
        row = lax.broadcasted_iota(jnp.int32, (FRAMES, 128), 0)
        bias = jnp.where(row < len_ref[yh], 0.0, -1e30)
        k = qkv[1].astype(F32)
        for h in range(2):
            kx[h] = jnp.where(lane == 64 * (1 - h), bias, k).astype(BF)
        kt[...] = k.T.astype(BF)
        p1_take(0)
        q = qkv[0].astype(F32) * 0.125
        for h in range(2):
            mine = (lane // 64) == h
            qm[h] = jnp.where(mine, q, jnp.where(lane == 64 * (1 - h), 1.0, 0.0)).astype(BF)

    def weights_of(h):
        @pl.when(works)
        def _():
            def tile(i):
                cols = pl.ds(mo(i * TILE, TILE), TILE)
                s = lax.dot_general(kx[h], qm[h, cols, :], NT, preferred_element_type=F32)
                e = jnp.exp(s - jnp.max(s, axis=0, keepdims=True))
                pt[h, :, cols] = (e * (1.0 / jnp.sum(e, axis=0, keepdims=True))).astype(BF)

            loop(FRAMES // TILE, tile)

    weights_of(0)
    weights_of(1)

    def p2_copy(c):
        rows = pl.ds(mo(c * ROWS, ROWS), ROWS)
        return remote(ob.at[rows, :], att_r.at[yh, pair], s_p2, r_p2, ctx=c)

    def p2_start(c):
        @pl.when(c != me)
        def _():
            p2_copy(c).start()

        @pl.when(c == me)
        def _():
            pltpu.make_async_copy(ob.at[my_rows, :], att_r.at[yh, pair], r_p2).start()

    @pl.when(works)
    def _():
        p1_take(2)
        vt[...] = qkv[2].astype(F32).T.astype(BF)

        def tile(i):
            cols = pl.ds(mo(i * TILE, TILE), TILE)
            out = [
                jnp.dot(vt[64 * h:64 * h + 64, :], pt[h, :, cols], preferred_element_type=F32) for h in range(2)
            ]
            ob[cols, :] = jnp.concatenate(out, axis=0).T.astype(BF)
            loop(TILE // ROWS, lambda j: p2_start(i * (TILE // ROWS) + j))

        loop(FRAMES // TILE, tile)

    def w_forward(i):
        c = 2 * i + core

        @pl.when(((c - me) * (c - ypart)) != 0)
        def _():
            arrived(w_rows(c), r_w.at[c])

        w_sib(i).start()

    loop(8, w_forward)

    def w_last(i):
        c = 2 * i + (1 - core)
        arrived(w_rows(c), r_w.at[c])

    loop(8, w_last)
    arrived(att_r, r_p2)
    for u in range(2):
        for p in range(PAIRS):
            att[64 * u:64 * u + 64, 128 * p:128 * p + 128] = att_r[u, p]

    frame = lax.broadcasted_iota(jnp.int32, (ROWS, TILE), 0) + me * ROWS
    before, after = me > 0, me < N_CTX - 1
    col_tiles = D // TILE

    def edge_copies(src, buf, base, i):
        cols = pl.ds(mo(i * TILE, TILE), TILE)
        up = remote(
            src.at[:, 48:64, cols], buf.at[0, :, :, cols], s_h.at[base + i], r_h.at[base + i],
            ctx=lax.rem(me + 1, N_CTX),
        )
        down = remote(
            src.at[:, 0:16, cols], buf.at[1, :, :, cols], s_h.at[base + 6 + i], r_h.at[base + 6 + i],
            ctx=lax.rem(me + N_CTX - 1, N_CTX),
        )
        return up, down

    def edges_do(src, buf, base, i, what):
        up, down = edge_copies(src, buf, base, i)

        @pl.when(after)
        def _():
            what(up)

        @pl.when(before)
        def _():
            what(down)

    def edges_take(buf, base, padded, i):
        cols = pl.ds(mo(i * TILE, TILE), TILE)
        for side, first, inner in ((0, 0, before), (1, 80, after)):
            @pl.when(inner)
            def _():
                arrived(buf.at[side, :, :, cols], r_h.at[base + 6 * side + i])
                padded[:, first:first + 16, cols] = buf[side, :, :, cols].astype(F32)

            @pl.when(jnp.logical_not(inner))
            def _():
                padded[:, first:first + 16, cols] = jnp.zeros((2, 16, TILE), F32)

    def rolled_by(block, r):
        return block if r == 0 else pltpu.roll(block, 96 - r, 0)

    for load in loads:
        load.wait()

    def project(i):
        cols = pl.ds(mo(i * TILE, TILE), TILE)
        out = lax.dot_general(att[...], w_full[cols, :], NT, preferred_element_type=F32)
        for u in range(2):
            h = (out[64 * u:64 * u + 64, :] + x_v[u, :, cols].astype(F32)).astype(BF).astype(F32)
            masked = jnp.where(frame < len_ref[u], h, 0.0)
            hid[u, :, cols] = h
            hb[u, :, cols] = masked.astype(BF)
            hp[u, 16:80, cols] = masked
        edges_do(hb, halo, 0, i, lambda copy: copy.start())

    loop(col_tiles, project)

    def conv_forward(i):
        edges_take(halo, 0, hp, i)
        for half in range(2):
            cols = pl.ds(mo(i * TILE + half * 128, 128), 128)
            w = taps[:, cols]
            for u in range(2):
                block = hp[u, :, cols]
                acc = jnp.zeros((ROWS, 128), F32)
                for r in range(8):
                    moved = rolled_by(block, r)
                    for a in range(4):
                        j = 8 * a + r - 1
                        if 0 <= j < TAPS:
                            acc = acc + w[j:j + 1, :] * moved[8 * a:8 * a + ROWS, :]
                sg = jax.nn.sigmoid(acc)
                bo_ref[u, :, cols] = (hid[u, :, cols] + acc * sg).astype(BF)
                gc = (go_v[u, :, cols].astype(F32) * (sg * (1.0 + acc * (1.0 - sg)))).astype(BF)
                gcb[u, :, cols] = gc
                gp[u, 16:80, cols] = gc.astype(F32)
        edges_do(gcb, ghalo, 12, i, lambda copy: copy.start())

    loop(col_tiles, conv_forward)

    def taps_gradient(i):
        cols = pl.ds(mo(i * 128, 128), 128)
        blocks = [hp[u, :, cols] for u in range(2)]
        grads = [gp[u, 16:80, cols] for u in range(2)]
        for r in range(8):
            moved = [rolled_by(block, r) for block in blocks]
            for a in range(4):
                j = 8 * a + r - 1
                if 0 <= j < TAPS:
                    total = sum(g * m[8 * a:8 * a + ROWS, :] for g, m in zip(grads, moved))
                    tgs[j:j + 1, cols] = jnp.sum(total, axis=0, keepdims=True)

    loop(CONV_BLOCKS, taps_gradient)
    frame_c = lax.broadcasted_iota(jnp.int32, (ROWS, 128), 0) + me * ROWS

    def conv_backward(i):
        edges_take(ghalo, 12, gp, i)
        for half in range(2):
            cols = pl.ds(mo(i * TILE + half * 128, 128), 128)
            w = taps[:, cols]
            for u in range(2):
                block = gp[u, :, cols]
                acc = jnp.zeros((ROWS, 128), F32)
                for r in range(8):
                    moved = rolled_by(block, r)
                    for a in range(4):
                        j = 31 - (8 * a + r)
                        if 0 <= j < TAPS:
                            acc = acc + w[j:j + 1, :] * moved[8 * a:8 * a + ROWS, :]
                gi = go_v[u, :, cols].astype(F32) + jnp.where(frame_c < len_ref[u], acc, 0.0)
                gi_ref[u, :, cols] = gi.astype(BF)

    loop(col_tiles, conv_backward)

    def p3_copy(n):
        return remote(
            ga_s.at[n // PAIRS, n % PAIRS], ga_r.at[my_rows, :], s_p3, r_p3, ctx=target_of(n)
        )

    gi_rows = gi_ref[...].reshape(2 * ROWS, D)

    def p3_start(n):
        t = target_of(n)

        @pl.when(t != me)
        def _():
            p3_copy(n).start()

        @pl.when(t == me)
        def _():
            pltpu.make_async_copy(ga_s.at[n // PAIRS, n % PAIRS], ga_r.at[my_rows, :], r_p3).start()

    def cotangent(i):
        cols = pl.ds(mo(i * TILE, TILE), TILE)
        out = jnp.dot(gi_rows, w_full[:, cols], preferred_element_type=F32).astype(BF)
        for u in range(2):
            for half in range(2):
                ga_s[u, 2 * i + half] = out[64 * u:64 * u + 64, 128 * half:128 * half + 128]
        loop(4, lambda m: p3_start((m // 2) * PAIRS + 2 * i + m % 2))

    loop(HD // TILE, cotangent)

    tap_rows = tgs[...].T.reshape(N_DP, 48, 128)
    packed = [tap_rows[:, 0:16, :]] + [
        pltpu.roll(tap_rows[:, 16 * k:16 * k + 16, :].reshape(N_DP * 16, 128), 32 * k, 1).reshape(N_DP, 16, 128)
        for k in (1, 2)
    ]
    tms[...] = (packed[0] + packed[1] + packed[2]).astype(BF)

    def over_dp(src, zr, ys, yr, s_z, r_z, s_y, r_y):
        def first(i):
            to = z_peer(i)
            remote(src.at[pl.ds(to - yl, 4)], zr.at[zi], s_z, r_z, dp=to).start()

        def start():
            loop(7, first)
            pltpu.make_async_copy(src.at[four], zr.at[zi], r_z).start()

        def second(i):
            to = y_peer(i)
            remote(ys.at[to - 4 * zi], yr.at[yl], s_y, r_y, dp=to).start()

        def turn():
            arrived(zr, r_z)
            ys[...] = jnp.sum(zr[...].astype(F32), axis=0).astype(BF)
            loop(3, second)
            pltpu.make_async_copy(ys.at[yl], yr.at[yl], r_y).start()

        def end():
            arrived(yr, r_y)
            return jnp.sum(yr[...].astype(F32), axis=0)

        def sent():
            arrived(src.at[0:28], s_z)
            arrived(ys.at[0:3], s_y)

        return start, turn, end, sent

    td_start, td_turn, td_end, td_sent = over_dp(tms, tzr, tys, tyr, s_td, r_td, s_te, r_te)

    def dp_first(i):
        to = z_peer(i)
        remote(ms.at[:, pl.ds(to - yl, 4)], zr.at[zi], s_dp, r_dp, dp=to).start()

    def dp_start():
        loop(7, dp_first)
        pltpu.make_async_copy(ms.at[:, four], zr.at[zi], r_dp).start()

    def dp_second(i):
        yh_to, yl_to, to = ring_peer(i)
        remote(ys.at[yh_to, yl_to], yr.at[yh, yl], s_de, r_de, **to).start()

    def dp_turn():
        arrived(zr, r_dp)
        ys[...] = jnp.sum(zr[...].astype(F32), axis=0).astype(BF)
        loop(7, dp_second)
        pltpu.make_async_copy(ys.at[yh, yl], yr.at[yh, yl], r_de).start()

    def rs1_copy(i):
        return remote(
            pp.at[pl.ds(2 * i, 2), 1 - core], rs1.at[pl.ds(2 * i, 2)], s_rs1.at[i], r_rs1.at[i], ctx=sib
        )

    def panel(i):
        cols = pl.ds(mo(i * 384, 128), 384)
        gi_cols = jnp.concatenate([gi_ref[0, :, cols], gi_ref[1, :, cols]], axis=0)
        out = lax.dot_general(gi_cols, att[...], TN, preferred_element_type=F32)
        pp[pl.ds(2 * i, 2)] = out.reshape(2, 2, 96, HD).astype(BF)
        rs1_copy(i).start()

    loop(4, panel)
    td_start()

    def rs2_copy(i):
        return remote(rs2s.at[i], rs2.at[x], s_rs2.at[i], r_rs2.at[x], ctx=4 * i + 2 * yh + core)

    def rs2_start(i):
        two = pl.ds(2 * i, 2)
        arrived(rs1.at[two], r_rs1.at[i])
        total = pp[two, core].astype(F32) + rs1[two].astype(F32)

        @pl.when(i != x)
        def _():
            rs2s[i] = total.astype(BF)
            rs2_copy(i).start()

        @pl.when(i == x)
        def _():
            own2[...] = total

    loop(4, rs2_start)

    def p4_copy(a, c):
        rows = pl.ds(mo(c * ROWS, ROWS), ROWS)
        return remote(
            dbuf.at[a, rows, :], grad_r.at[a, yh, pair], s_p4, r_p4.at[a], ctx=c,
        )

    def p4_start(a, i):
        def one(j):
            c = i * (TILE // ROWS) + j

            @pl.when(c != me)
            def _():
                p4_copy(a, c).start()

            @pl.when(c == me)
            def _():
                pltpu.make_async_copy(dbuf.at[a, my_rows, :], grad_r.at[a, yh, pair], r_p4.at[a]).start()

        loop(TILE // ROWS, one)

    tile_lane = lax.broadcasted_iota(jnp.int32, (TILE, 128), 1) // 64

    @pl.when(works)
    def _():
        arrived(ga_r, r_p3)

        def values(i):
            rows = pl.ds(mo(i * TILE, TILE), TILE)
            first = jnp.dot(pt[0, rows, :], ga_r[...], preferred_element_type=F32)
            second = jnp.dot(pt[1, rows, :], ga_r[...], preferred_element_type=F32)
            dbuf[2, rows, :] = jnp.where(tile_lane == 0, first, second).astype(BF)
            p4_start(2, i)

        loop(FRAMES // TILE, values)

    def backward_tile(i):
        cols = pl.ds(mo(i * TILE, TILE), TILE)
        ga = ga_r[cols, :].astype(F32)
        prod = (ga * ob[cols, :].astype(F32)).T
        parts = []
        for h in range(2):
            gmb = jnp.where(tile_lane == h, ga, 0.0).astype(BF)
            delta = jnp.sum(prod[64 * h:64 * h + 64, :], axis=0, keepdims=True)
            dpt = lax.dot_general(qkv[2], gmb, NT, preferred_element_type=F32)
            dst = (pt[h, :, cols].astype(F32) * (dpt - delta)).astype(BF)
            ds[h, :, cols] = dst
            parts.append(jnp.dot(kt[64 * h:64 * h + 64, :], dst, preferred_element_type=F32))
        dbuf[0, cols, :] = (jnp.concatenate(parts, axis=0).T * 0.125).astype(BF)
        p4_start(0, i)

    def backward_half(first):
        @pl.when(works)
        def _():
            loop(2, lambda i: backward_tile(i + first))

    td_turn()

    def rs2_take(i):
        @pl.when(i != x)
        def _():
            arrived(rs2.at[i], r_rs2.at[i])
            own2[...] += rs2[i].astype(F32)

    loop(4, rs2_take)
    for y in range(2):
        own3[0:96, :] = own2[y]
        ms[y] = jnp.concatenate(
            [own3[...].T.reshape(N_DP, 24, 128), jnp.zeros((N_DP, 8, 128), F32)], axis=1
        ).astype(BF)
    dp_start()
    backward_half(0)

    def t_copy(c):
        return remote(th, tr.at[me], s_t, r_t, ctx=c)

    def t_start(i):
        t_copy(lax.rem(i + 1 + me, N_CTX)).start()

    th[...] = td_end().astype(BF)
    loop(N_CTX - 1, t_start)
    pltpu.make_async_copy(th, tr.at[me], r_t).start()
    backward_half(2)

    @pl.when(works)
    def _():
        for h in range(2):
            qm[h] = jnp.where((lane // 64) == h, qkv[0].astype(F32) * 0.125, 0.0).astype(BF)

        def keys(i):
            rows = pl.ds(mo(i * TILE, TILE), TILE)
            out = jnp.dot(ds[0, rows, :], qm[0], preferred_element_type=F32)
            out = out + jnp.dot(ds[1, rows, :], qm[1], preferred_element_type=F32)
            dbuf[1, rows, :] = out.astype(BF)
            p4_start(1, i)

        loop(FRAMES // TILE, keys)

    dp_turn()

    def p4_take(a):
        arrived(grad_r.at[a], r_p4.at[a])

    for a, out in ((2, gv_ref), (0, gq_ref), (1, gk_ref)):
        p4_take(a)
        for u in range(2):
            for p in range(PAIRS):
                out[u, :, 128 * p:128 * p + 128] = grad_r[a, u, p]

    arrived(tr, r_t)
    gt_ref[...] = jnp.sum(tr[...].astype(F32), axis=0)
    arrived(yr, r_de)
    gw_ref[...] = jnp.sum(yr[...].astype(F32).reshape(8, 32, 128), axis=0)

    arrived(w_a.at[0, 0:7], s_ay)
    arrived(w_a.at[:, 0:28], s_az)
    td_sent()
    arrived(ms.at[:, 0:28], s_dp)
    arrived(w_a.at[0, 0:7], s_de)
    arrived(tr.at[0:N_CTX - 1], s_t)
    others = ROWS * (N_CTX - 1)

    @pl.when(works)
    def _():
        arrived(qkv.at[:, 0:ROWS * (TARGETS - 1), :], s_p1)
        arrived(ga_r.at[0:ROWS * (TARGETS - 1), :], s_p3)
        arrived(ob.at[0:others, :], s_p2)
        arrived(dbuf.at[:, 0:others, :], s_p4)

    @pl.when(jnp.logical_not(works))
    def _():
        arrived(qkv.at[:, 0:ROWS * TARGETS, :], s_p1)
        arrived(ga_r.at[0:ROWS * TARGETS, :], s_p3)


    def sent_x(i):
        @pl.when(i != x)
        def _():
            w_x(i, 0).wait_send()
            w_x(i, 1).wait_send()
            rs2_copy(i).wait_send()

        rs1_copy(i).wait_send()

    loop(4, sent_x)
    loop(8, lambda i: w_sib(i).wait_send())
    for src, buf, base in ((hb, halo, 0), (gcb, ghalo, 12)):
        loop(col_tiles, lambda i: edges_do(src, buf, base, i, lambda copy: copy.wait_send()))


def finish(
    bo, gi, gq, gk, gv, gw_ref, gt_ref, bo_o, gi_o, gq_o, gk_o, gv_o, gw_o, gt_o,
    bo_v, gi_v, gq_v, gk_v, gv_v, gw_v, gt_v, in_sems, out_sems,
):
    held = (bo_v, gi_v, gq_v, gk_v, gv_v, gw_v, gt_v)
    outs = (bo_o, gi_o, gq_o, gk_o, gv_o, gw_o, gt_o)
    loads = [pltpu.make_async_copy(a, b, in_sems.at[i]) for i, (a, b) in enumerate(zip((bo, gi, gq, gk, gv), held))]
    stores = [pltpu.make_async_copy(a, b, out_sems.at[i]) for i, (a, b) in enumerate(zip(held, outs))]
    for load in loads:
        load.start()
    gw_v[...] = gw_ref[0:24, 0:96]
    stores[5].start()
    wide = jnp.concatenate([gt_ref[...], jnp.zeros((112, 128), F32)], axis=0).T
    gt_v[...] = jnp.concatenate([wide[32 * k:32 * k + TAPS, 0:16] for k in range(3)], axis=1)
    stores[6].start()
    for load, store in zip(loads, stores):
        load.wait()
        store.start()
    for store in stores:
        store.wait()


def per_device(frame_input, queries, key_proj, value_proj, out_weight, conv_weight, lengths, grad_output):
    vmem = pl.BlockSpec(memory_space=pltpu.VMEM)
    hbm = pl.BlockSpec(memory_space=pltpu.HBM)
    dma = lambda n: pltpu.SemaphoreType.DMA((n,))
    scratch = [
        ((2, ROWS, D), BF), ((2, ROWS, D), BF),
        ((3, FRAMES, 128), BF), ((2, FRAMES, 128), BF), ((2, FRAMES, 128), BF), ((128, FRAMES), BF),
        ((128, FRAMES), BF), ((2, FRAMES, FRAMES), BF), ((2, FRAMES, FRAMES), BF),
        ((FRAMES, 128), BF), ((2, PAIRS, ROWS, 128), BF), ((2 * ROWS, HD), BF), ((2, PAIRS, ROWS, 128), BF),
        ((FRAMES, 128), BF), ((3, FRAMES, 128), BF), ((3, 2, PAIRS, ROWS, 128), BF),
        ((2, N_DP, 32, 128), BF), ((32, D), F32), ((D, HD), BF), ((32, 128), BF),
        ((2, ROWS, D), F32), ((2, ROWS, D), BF), ((2, 2, 16, D), BF), ((2, 96, D), F32),
        ((2, ROWS, D), BF), ((2, 2, 16, D), BF), ((2, 96, D), F32), ((128, D), F32),
        ((8, 2, 96, HD), BF), ((8, 96, HD), BF), ((4, 2, 96, HD), BF), ((4, 2, 96, HD), BF),
        ((2, 96, HD), F32), ((128, HD), F32),
        ((2, N_DP, 32, 128), BF), ((8, 2, 4, 32, 128), BF), ((2, 4, 32, 128), BF), ((2, 4, 32, 128), BF),
        ((N_DP, 16, 128), BF), ((8, 4, 16, 128), BF), ((4, 16, 128), BF), ((4, 16, 128), BF),
        ((16, 128), BF), ((N_CTX, 16, 128), BF),
    ]
    one = pltpu.SemaphoreType.DMA
    sems = [
        dma(2), one, dma(3), one, one, one, dma(8), dma(17), dma(16), one, one, dma(24), dma(24), one, one, one,
        dma(3), dma(4), dma(4), dma(4), dma(4), one, one, one, one, one, one, one, one, one, one,
    ]
    shapes = (
        ((2, ROWS, D), BF), ((2, ROWS, D), BF), ((2, ROWS, HD), BF), ((2, ROWS, HD), BF), ((2, ROWS, HD), BF),
        ((32, 128), F32), ((16, 128), F32),
    )
    bo, gi, gq, gk, gv, gw, gt = pl.pallas_call(
        kernel,
        out_shape=[jax.ShapeDtypeStruct(s, t) for s, t in shapes],
        in_specs=[pl.BlockSpec(memory_space=pltpu.SMEM)] + [hbm] * 4 + [vmem, vmem, hbm],
        out_specs=[vmem] * 7,
        scratch_shapes=[pltpu.VMEM(s, t) for s, t in scratch] + sems,
        compiler_params=pltpu.CompilerParams(
            collective_id=0, has_side_effects=True, vmem_limit_bytes=60 * 1024 * 1024
        ),
        cost_estimate=pl.CostEstimate(flops=3 * 10**9, bytes_accessed=4 * 10**6, transcendentals=2 * 10**6),
    )(lengths, frame_input, queries, key_proj, value_proj, out_weight.T, conv_weight, grad_output)
    final = shapes[0:5] + (((24, 96), F32), ((TAPS, 48), F32))
    bo, gi, gq, gk, gv, gw, gt = (
        pl.pallas_call(
            finish,
            out_shape=[jax.ShapeDtypeStruct(s, t) for s, t in final],
            in_specs=[hbm] * 5 + [vmem] * 2,
            out_specs=[hbm] * 7,
            scratch_shapes=[pltpu.VMEM(s, t) for s, t in final] + [dma(5), dma(7)],
            compiler_params=pltpu.CompilerParams(vmem_limit_bytes=60 * 1024 * 1024),
            cost_estimate=pl.CostEstimate(flops=10**5, bytes_accessed=3 * 10**6, transcendentals=0),
        )(bo, gi, gq, gk, gv, gw, gt)
    )
    return bo, gi, gq, gk, gv, gw.T, gt


def solution(mesh):
    rows = P("dp", "ctx", None)
    return jax.shard_map(
        per_device,
        mesh=mesh,
        in_specs=(rows, rows, rows, rows, P("ctx", "dp"), P(None, "dp"), P("dp"), rows),
        out_specs=(rows, rows, rows, rows, rows, P("ctx", "dp"), P(None, "dp")),
        check_vma=False,
    )
```

```python
import jax
import jax.numpy as jnp
from jax import lax
from jax.experimental import pallas as pl
from jax.experimental.pallas import tpu as pltpu
from jax.sharding import PartitionSpec as P

BF = jnp.bfloat16
F32 = jnp.float32
N_CTX = 16
N_DP = 32
ROWS = 64
FRAMES = 1024
D = 1536
HD = 768
PAIRS = 6
TARGETS = 2 * PAIRS
TAPS = 31
TILE = 256
CONV_BLOCKS = D // 128
NT = (((1,), (1,)), ((), ()))
TN = (((0,), (0,)), ((), ()))


def target_of(n):
    u, p = n // PAIRS, n % PAIRS
    hi = p // 4
    x = (1 - hi) * p + hi * (2 * (p - 4) + u)
    return 4 * x + 2 * u + hi


def remote(src, dst, send, recv, **axis):
    return pltpu.make_async_remote_copy(
        src_ref=src,
        dst_ref=dst,
        send_sem=send,
        recv_sem=recv,
        device_id=axis,
        device_id_type=pl.DeviceIdType.MESH,
    )


def arrived(dst, sem):
    pltpu.make_async_copy(dst, dst, sem).wait()


def loop(count, body):
    def step(i, carry):
        body(i)
        return carry

    lax.fori_loop(0, count, step, 0)


def mo(value, unit):
    return pl.multiple_of(value, unit)


def kernel(
    len_ref, x_ref, q_ref, k_ref, v_ref, wt_ref, cw_ref, go_ref,
    bo_ref, gi_ref, gq_ref, gk_ref, gv_ref, gw_ref, gt_ref,
    x_v, go_v, qkv, kx, qm, kt, vt, pt, ds, ob, att_r, att, ga_s, ga_r, dbuf, grad_r,
    w_a, taps, w_full, msg_ref,
    hid, hb, halo, hp, gcb, ghalo, gp, tgs,
    pp, rs1, rs2s, rs2, own2, own3, ms, zr, ys, yr, tms, tzr, tys, tyr, th, tr,
    s_in, s_p1, r_p1, s_ay, r_ay, s_az, r_az, s_w, r_w, s_p2, r_p2, s_h, r_h, s_p3, r_p3, s_p4, r_p4,
    s_rs1, r_rs1, s_rs2, r_rs2, s_dp, r_dp, s_de, r_de, s_td, r_td, s_te, r_te, s_t, r_t,
):
    me = lax.axis_index("ctx")
    dp = lax.axis_index("dp")
    x = me // 4
    yh = (me // 2) % 2
    core = me % 2
    sib = 4 * x + 2 * yh + (1 - core)
    ypart = 4 * x + 2 * (1 - yh) + core
    pair = (1 - core) * x + core * (4 + x // 2)
    works = (core * ((x + yh) % 2)) == 0
    zi, yl = dp // 4, dp % 4
    my_rows = pl.ds(mo(me * ROWS, ROWS), ROWS)
    inputs = (q_ref, k_ref, v_ref)

    loads = [pltpu.make_async_copy(a, b, s_in.at[i]) for i, (a, b) in enumerate(((x_ref, x_v), (go_ref, go_v)))]
    for load in loads:
        load.start()

    wide = jnp.concatenate([cw_ref[...].astype(F32), jnp.zeros((TAPS, 80), F32)], axis=1)
    right = jnp.concatenate([wide, jnp.zeros((128 - TAPS, 128), F32)], axis=0).T[0:48, 0:32]
    top = jnp.concatenate([wt_ref[...].astype(F32), right[0:24]], axis=1)
    low = jnp.concatenate([right[24:32], right[32:40], right[40:48], jnp.zeros((8, 32), F32)], axis=1)
    msg_ref[...] = jnp.concatenate([top, low], axis=0).astype(BF)

    barrier = pltpu.get_barrier_semaphore()

    def greet_ctx(i):
        @pl.when(i != me)
        def _():
            pl.semaphore_signal(barrier, inc=1, device_id={"ctx": i}, device_id_type=pl.DeviceIdType.MESH)

    def z_peer(i):
        return 4 * lax.rem(zi + 1 + i, 8) + yl

    def y_peer(i):
        return 4 * zi + lax.rem(yl + 1 + i, 4)

    def ring_peer(i):
        o = lax.rem(4 * yh + yl + 1 + i, 8)
        return o // 4, o % 4, {"ctx": 4 * x + 2 * (o // 4) + core, "dp": 4 * zi + o % 4}

    def greet(to):
        pl.semaphore_signal(barrier, inc=1, device_id=to, device_id_type=pl.DeviceIdType.MESH)

    loop(N_CTX, greet_ctx)
    loop(7, lambda i: greet({"dp": z_peer(i)}))
    loop(7, lambda i: greet(ring_peer(i)[2]))
    pl.semaphore_wait(barrier, N_CTX - 1 + 7 + 7)

    def p1_parts(a, n):
        src = inputs[a].at[n // PAIRS, :, pl.ds(mo((n % PAIRS) * 128, 128), 128)]
        return src, qkv.at[a, my_rows, :]

    def p1_copy(a, n):
        src, dst = p1_parts(a, n)
        return remote(src, dst, s_p1, r_p1.at[a], ctx=target_of(n))

    def p1_start(a, u):
        def one(i):
            n = u * PAIRS + lax.rem(i + me, PAIRS)
            t = target_of(n)

            @pl.when(t != me)
            def _():
                p1_copy(a, n).start()

            @pl.when(t == me)
            def _():
                src, dst = p1_parts(a, n)
                pltpu.make_async_copy(src, dst, r_p1.at[a]).start()

        loop(PAIRS, one)

    four = pl.ds(4 * zi, 4)

    def a_y(i):
        remote(msg_ref, w_a.at[yh, dp], s_ay, r_ay, **ring_peer(i)[2]).start()

    def a_z(i):
        remote(w_a.at[:, four], w_a.at[:, four], s_az, r_az.at[zi], dp=z_peer(i)).start()

    def a_z_take(i):
        source = lax.rem(zi + 1 + i, 8)
        arrived(w_a.at[:, pl.ds(4 * source, 4)], r_az.at[source])

    loop(7, a_y)
    pltpu.make_async_copy(msg_ref, w_a.at[yh, dp], r_ay).start()
    p1_start(1, 1 - yh)
    p1_start(0, 1 - yh)
    arrived(w_a.at[:, four], r_ay)
    loop(7, a_z)
    p1_start(1, yh)
    p1_start(0, yh)
    p1_start(2, 1 - yh)
    p1_start(2, yh)
    tgs[...] = jnp.zeros_like(tgs)
    own3[...] = jnp.zeros_like(own3)
    loop(7, a_z_take)
    for y in range(2):
        pieces = w_a[y].astype(F32)
        block = pieces[:, 0:24, :].reshape(HD, 128).T
        w_full[pl.ds(mo((4 * x + 2 * y + core) * 96, 32), 96), :] = block[0:96, :].astype(BF)
        if y == 0:
            rest = pieces[:, 24:32, :].reshape(N_DP * 8, 128)
            moved_rest = [pltpu.roll(rest, 96 - 32 * k, 1).reshape(N_DP, 8, 128) for k in range(3)]
            taps[...] = jnp.concatenate([pieces[:, 0:24, :]] + moved_rest, axis=1).reshape(D, 128).T[96:128, :]

    def w_rows(c):
        return w_full.at[pl.ds(mo(c * 96, 32), 96), :]

    def w_copy(c, slot, to):
        return remote(w_rows(c), w_rows(c), s_w.at[slot], r_w.at[c], ctx=to)

    def w_x(i, y):
        return w_copy(4 * x + 2 * y + core, 1 + 4 * y + i, 4 * i + 2 * yh + core)

    def w_sib(i):
        return w_copy(2 * i + core, 9 + i, sib)

    def w_x_start(y):
        def one(i):
            @pl.when(i != x)
            def _():
                w_x(i, y).start()

        loop(4, one)

    w_x_start(0)
    w_x_start(1)

    lane = lax.broadcasted_iota(jnp.int32, (FRAMES, 128), 1)

    def p1_take(a):
        arrived(qkv.at[a], r_p1.at[a])

    @pl.when(works)
    def _():
        p1_take(1)
        row = lax.broadcasted_iota(jnp.int32, (FRAMES, 128), 0)
        bias = jnp.where(row < len_ref[yh], 0.0, -1e30)
        k = qkv[1].astype(F32)
        for h in range(2):
            kx[h] = jnp.where(lane == 64 * (1 - h), bias, k).astype(BF)
        kt[...] = k.T.astype(BF)
        p1_take(0)
        q = qkv[0].astype(F32) * 0.125
        for h in range(2):
            mine = (lane // 64) == h
            qm[h] = jnp.where(mine, q, jnp.where(lane == 64 * (1 - h), 1.0, 0.0)).astype(BF)

    def weights_of(h):
        @pl.when(works)
        def _():
            def tile(i):
                cols = pl.ds(mo(i * TILE, TILE), TILE)
                s = lax.dot_general(kx[h], qm[h, cols, :], NT, preferred_element_type=F32)
                e = jnp.exp(s - jnp.max(s, axis=0, keepdims=True))
                pt[h, :, cols] = (e * (1.0 / jnp.sum(e, axis=0, keepdims=True))).astype(BF)

            loop(FRAMES // TILE, tile)

    weights_of(0)
    weights_of(1)

    def p2_copy(c):
        rows = pl.ds(mo(c * ROWS, ROWS), ROWS)
        return remote(ob.at[rows, :], att_r.at[yh, pair], s_p2, r_p2, ctx=c)

    def p2_start(c):
        @pl.when(c != me)
        def _():
            p2_copy(c).start()

        @pl.when(c == me)
        def _():
            pltpu.make_async_copy(ob.at[my_rows, :], att_r.at[yh, pair], r_p2).start()

    @pl.when(works)
    def _():
        p1_take(2)
        vt[...] = qkv[2].astype(F32).T.astype(BF)

        def tile(i):
            cols = pl.ds(mo(i * TILE, TILE), TILE)
            out = [
                jnp.dot(vt[64 * h:64 * h + 64, :], pt[h, :, cols], preferred_element_type=F32) for h in range(2)
            ]
            ob[cols, :] = jnp.concatenate(out, axis=0).T.astype(BF)
            loop(TILE // ROWS, lambda j: p2_start(i * (TILE // ROWS) + j))

        loop(FRAMES // TILE, tile)

    def w_forward(i):
        c = 2 * i + core

        @pl.when(((c - me) * (c - ypart)) != 0)
        def _():
            arrived(w_rows(c), r_w.at[c])

        w_sib(i).start()

    loop(8, w_forward)

    def w_last(i):
        c = 2 * i + (1 - core)
        arrived(w_rows(c), r_w.at[c])

    loop(8, w_last)
    arrived(att_r, r_p2)
    for u in range(2):
        for p in range(PAIRS):
            att[64 * u:64 * u + 64, 128 * p:128 * p + 128] = att_r[u, p]

    frame = lax.broadcasted_iota(jnp.int32, (ROWS, TILE), 0) + me * ROWS
    before, after = me > 0, me < N_CTX - 1
    col_tiles = D // TILE

    def edge_copies(src, buf, base, i):
        cols = pl.ds(mo(i * TILE, TILE), TILE)
        up = remote(
            src.at[:, 48:64, cols], buf.at[0, :, :, cols], s_h.at[base + i], r_h.at[base + i],
            ctx=lax.rem(me + 1, N_CTX),
        )
        down = remote(
            src.at[:, 0:16, cols], buf.at[1, :, :, cols], s_h.at[base + 6 + i], r_h.at[base + 6 + i],
            ctx=lax.rem(me + N_CTX - 1, N_CTX),
        )
        return up, down

    def edges_do(src, buf, base, i, what):
        up, down = edge_copies(src, buf, base, i)

        @pl.when(after)
        def _():
            what(up)

        @pl.when(before)
        def _():
            what(down)

    def edges_take(buf, base, padded, i):
        cols = pl.ds(mo(i * TILE, TILE), TILE)
        for side, first, inner in ((0, 0, before), (1, 80, after)):
            @pl.when(inner)
            def _():
                arrived(buf.at[side, :, :, cols], r_h.at[base + 6 * side + i])
                padded[:, first:first + 16, cols] = buf[side, :, :, cols].astype(F32)

            @pl.when(jnp.logical_not(inner))
            def _():
                padded[:, first:first + 16, cols] = jnp.zeros((2, 16, TILE), F32)

    def rolled_by(block, r):
        return block if r == 0 else pltpu.roll(block, 96 - r, 0)

    for load in loads:
        load.wait()

    def project(i):
        cols = pl.ds(mo(i * TILE, TILE), TILE)
        out = lax.dot_general(att[...], w_full[cols, :], NT, preferred_element_type=F32)
        for u in range(2):
            h = (out[64 * u:64 * u + 64, :] + x_v[u, :, cols].astype(F32)).astype(BF).astype(F32)
            masked = jnp.where(frame < len_ref[u], h, 0.0)
            hid[u, :, cols] = h
            hb[u, :, cols] = masked.astype(BF)
            hp[u, 16:80, cols] = masked
        edges_do(hb, halo, 0, i, lambda copy: copy.start())

    loop(col_tiles, project)

    def conv_forward(i):
        edges_take(halo, 0, hp, i)
        for half in range(2):
            cols = pl.ds(mo(i * TILE + half * 128, 128), 128)
            w = taps[:, cols]
            for u in range(2):
                block = hp[u, :, cols]
                acc = jnp.zeros((ROWS, 128), F32)
                for r in range(8):
                    moved = rolled_by(block, r)
                    for a in range(4):
                        j = 8 * a + r - 1
                        if 0 <= j < TAPS:
                            acc = acc + w[j:j + 1, :] * moved[8 * a:8 * a + ROWS, :]
                sg = jax.nn.sigmoid(acc)
                bo_ref[u, :, cols] = (hid[u, :, cols] + acc * sg).astype(BF)
                gc = (go_v[u, :, cols].astype(F32) * (sg * (1.0 + acc * (1.0 - sg)))).astype(BF)
                gcb[u, :, cols] = gc
                gp[u, 16:80, cols] = gc.astype(F32)
        edges_do(gcb, ghalo, 12, i, lambda copy: copy.start())

    loop(col_tiles, conv_forward)

    def taps_gradient(i):
        cols = pl.ds(mo(i * 128, 128), 128)
        blocks = [hp[u, :, cols] for u in range(2)]
        grads = [gp[u, 16:80, cols] for u in range(2)]
        for r in range(8):
            moved = [rolled_by(block, r) for block in blocks]
            for a in range(4):
                j = 8 * a + r - 1
                if 0 <= j < TAPS:
                    total = sum(g * m[8 * a:8 * a + ROWS, :] for g, m in zip(grads, moved))
                    tgs[j:j + 1, cols] = jnp.sum(total, axis=0, keepdims=True)

    frame_c = lax.broadcasted_iota(jnp.int32, (ROWS, 128), 0) + me * ROWS

    def conv_backward(i):
        edges_take(ghalo, 12, gp, i)
        for half in range(2):
            cols = pl.ds(mo(i * TILE + half * 128, 128), 128)
            w = taps[:, cols]
            for u in range(2):
                block = gp[u, :, cols]
                acc = jnp.zeros((ROWS, 128), F32)
                for r in range(8):
                    moved = rolled_by(block, r)
                    for a in range(4):
                        j = 31 - (8 * a + r)
                        if 0 <= j < TAPS:
                            acc = acc + w[j:j + 1, :] * moved[8 * a:8 * a + ROWS, :]
                gi = go_v[u, :, cols].astype(F32) + jnp.where(frame_c < len_ref[u], acc, 0.0)
                gi_ref[u, :, cols] = gi.astype(BF)

    loop(col_tiles, conv_backward)

    def p3_copy(n):
        return remote(
            ga_s.at[n // PAIRS, n % PAIRS], ga_r.at[my_rows, :], s_p3, r_p3, ctx=target_of(n)
        )

    gi_rows = gi_ref[...].reshape(2 * ROWS, D)

    def p3_start(n):
        t = target_of(n)

        @pl.when(t != me)
        def _():
            p3_copy(n).start()

        @pl.when(t == me)
        def _():
            pltpu.make_async_copy(ga_s.at[n // PAIRS, n % PAIRS], ga_r.at[my_rows, :], r_p3).start()

    def cotangent(i):
        cols = pl.ds(mo(i * TILE, TILE), TILE)
        out = jnp.dot(gi_rows, w_full[:, cols], preferred_element_type=F32).astype(BF)
        for u in range(2):
            for half in range(2):
                ga_s[u, 2 * i + half] = out[64 * u:64 * u + 64, 128 * half:128 * half + 128]
        loop(4, lambda m: p3_start((m // 2) * PAIRS + 2 * i + m % 2))

    loop(HD // TILE, cotangent)

    def over_dp(src, zr, ys, yr, s_z, r_z, s_y, r_y):
        def first(i):
            to = z_peer(i)
            remote(src.at[pl.ds(to - yl, 4)], zr.at[zi], s_z, r_z, dp=to).start()

        def start():
            loop(7, first)
            pltpu.make_async_copy(src.at[four], zr.at[zi], r_z).start()

        def second(i):
            to = y_peer(i)
            remote(ys.at[to - 4 * zi], yr.at[yl], s_y, r_y, dp=to).start()

        def turn():
            arrived(zr, r_z)
            ys[...] = jnp.sum(zr[...].astype(F32), axis=0).astype(BF)
            loop(3, second)
            pltpu.make_async_copy(ys.at[yl], yr.at[yl], r_y).start()

        def end():
            arrived(yr, r_y)
            return jnp.sum(yr[...].astype(F32), axis=0)

        def sent():
            arrived(src.at[0:28], s_z)
            arrived(ys.at[0:3], s_y)

        return start, turn, end, sent

    td_start, td_turn, td_end, td_sent = over_dp(tms, tzr, tys, tyr, s_td, r_td, s_te, r_te)

    def dp_first(i):
        to = z_peer(i)
        remote(ms.at[:, pl.ds(to - yl, 4)], zr.at[zi], s_dp, r_dp, dp=to).start()

    def dp_start():
        loop(7, dp_first)
        pltpu.make_async_copy(ms.at[:, four], zr.at[zi], r_dp).start()

    def dp_second(i):
        yh_to, yl_to, to = ring_peer(i)
        remote(ys.at[yh_to, yl_to], yr.at[yh, yl], s_de, r_de, **to).start()

    def dp_turn():
        arrived(zr, r_dp)
        ys[...] = jnp.sum(zr[...].astype(F32), axis=0).astype(BF)
        loop(7, dp_second)
        pltpu.make_async_copy(ys.at[yh, yl], yr.at[yh, yl], r_de).start()

    def rs1_copy(i):
        return remote(
            pp.at[pl.ds(2 * i, 2), 1 - core], rs1.at[pl.ds(2 * i, 2)], s_rs1.at[i], r_rs1.at[i], ctx=sib
        )

    def panel(i):
        cols = pl.ds(mo(i * 384, 128), 384)
        gi_cols = jnp.concatenate([gi_ref[0, :, cols], gi_ref[1, :, cols]], axis=0)
        out = lax.dot_general(gi_cols, att[...], TN, preferred_element_type=F32)
        pp[pl.ds(2 * i, 2)] = out.reshape(2, 2, 96, HD).astype(BF)
        rs1_copy(i).start()

    loop(4, panel)

    def rs2_copy(i):
        return remote(rs2s.at[i], rs2.at[x], s_rs2.at[i], r_rs2.at[x], ctx=4 * i + 2 * yh + core)

    def rs2_start(i):
        two = pl.ds(2 * i, 2)
        arrived(rs1.at[two], r_rs1.at[i])
        total = pp[two, core].astype(F32) + rs1[two].astype(F32)

        @pl.when(i != x)
        def _():
            rs2s[i] = total.astype(BF)
            rs2_copy(i).start()

        @pl.when(i == x)
        def _():
            own2[...] = total

    loop(4, rs2_start)

    def p4_copy(a, c):
        rows = pl.ds(mo(c * ROWS, ROWS), ROWS)
        return remote(
            dbuf.at[a, rows, :], grad_r.at[a, yh, pair], s_p4, r_p4.at[a], ctx=c,
        )

    def p4_start(a, i):
        def one(j):
            c = i * (TILE // ROWS) + j

            @pl.when(c != me)
            def _():
                p4_copy(a, c).start()

            @pl.when(c == me)
            def _():
                pltpu.make_async_copy(dbuf.at[a, my_rows, :], grad_r.at[a, yh, pair], r_p4.at[a]).start()

        loop(TILE // ROWS, one)

    tile_lane = lax.broadcasted_iota(jnp.int32, (TILE, 128), 1) // 64

    @pl.when(works)
    def _():
        arrived(ga_r, r_p3)

        def values(i):
            rows = pl.ds(mo(i * TILE, TILE), TILE)
            first = jnp.dot(pt[0, rows, :], ga_r[...], preferred_element_type=F32)
            second = jnp.dot(pt[1, rows, :], ga_r[...], preferred_element_type=F32)
            dbuf[2, rows, :] = jnp.where(tile_lane == 0, first, second).astype(BF)
            p4_start(2, i)

        loop(FRAMES // TILE, values)

    def backward_tile(i):
        cols = pl.ds(mo(i * TILE, TILE), TILE)
        ga = ga_r[cols, :].astype(F32)
        prod = (ga * ob[cols, :].astype(F32)).T
        parts = []
        for h in range(2):
            gmb = jnp.where(tile_lane == h, ga, 0.0).astype(BF)
            delta = jnp.sum(prod[64 * h:64 * h + 64, :], axis=0, keepdims=True)
            dpt = lax.dot_general(qkv[2], gmb, NT, preferred_element_type=F32)
            dst = (pt[h, :, cols].astype(F32) * (dpt - delta)).astype(BF)
            ds[h, :, cols] = dst
            parts.append(jnp.dot(kt[64 * h:64 * h + 64, :], dst, preferred_element_type=F32))
        dbuf[0, cols, :] = (jnp.concatenate(parts, axis=0).T * 0.125).astype(BF)
        p4_start(0, i)

    def backward_half(first):
        @pl.when(works)
        def _():
            loop(2, lambda i: backward_tile(i + first))

    loop(CONV_BLOCKS, taps_gradient)
    tap_rows = tgs[...].T.reshape(N_DP, 48, 128)
    packed = [tap_rows[:, 0:16, :]] + [
        pltpu.roll(tap_rows[:, 16 * k:16 * k + 16, :].reshape(N_DP * 16, 128), 32 * k, 1).reshape(N_DP, 16, 128)
        for k in (1, 2)
    ]
    tms[...] = (packed[0] + packed[1] + packed[2]).astype(BF)
    td_start()

    def rs2_take(i):
        @pl.when(i != x)
        def _():
            arrived(rs2.at[i], r_rs2.at[i])
            own2[...] += rs2[i].astype(F32)

    loop(4, rs2_take)
    for y in range(2):
        own3[0:96, :] = own2[y]
        ms[y] = jnp.concatenate(
            [own3[...].T.reshape(N_DP, 24, 128), jnp.zeros((N_DP, 8, 128), F32)], axis=1
        ).astype(BF)
    dp_start()
    backward_half(0)

    td_turn()
    backward_half(2)

    @pl.when(works)
    def _():
        for h in range(2):
            qm[h] = jnp.where((lane // 64) == h, qkv[0].astype(F32) * 0.125, 0.0).astype(BF)

        def keys(i):
            rows = pl.ds(mo(i * TILE, TILE), TILE)
            out = jnp.dot(ds[0, rows, :], qm[0], preferred_element_type=F32)
            out = out + jnp.dot(ds[1, rows, :], qm[1], preferred_element_type=F32)
            dbuf[1, rows, :] = out.astype(BF)
            p4_start(1, i)

        loop(FRAMES // TILE, keys)

    dp_turn()

    def t_copy(c):
        return remote(th, tr.at[me], s_t, r_t, ctx=c)

    def t_start(i):
        t_copy(lax.rem(i + 1 + me, N_CTX)).start()

    th[...] = td_end().astype(BF)
    loop(N_CTX - 1, t_start)
    pltpu.make_async_copy(th, tr.at[me], r_t).start()

    def p4_take(a):
        arrived(grad_r.at[a], r_p4.at[a])

    for a, out in ((2, gv_ref), (0, gq_ref), (1, gk_ref)):
        p4_take(a)
        for u in range(2):
            for p in range(PAIRS):
                out[u, :, 128 * p:128 * p + 128] = grad_r[a, u, p]

    arrived(tr, r_t)
    gt_ref[...] = jnp.sum(tr[...].astype(F32), axis=0)
    arrived(yr, r_de)
    gw_ref[...] = jnp.sum(yr[...].astype(F32).reshape(8, 32, 128), axis=0)

    arrived(w_a.at[0, 0:7], s_ay)
    arrived(w_a.at[:, 0:28], s_az)
    td_sent()
    arrived(ms.at[:, 0:28], s_dp)
    arrived(w_a.at[0, 0:7], s_de)
    arrived(tr.at[0:N_CTX - 1], s_t)
    others = ROWS * (N_CTX - 1)

    @pl.when(works)
    def _():
        arrived(qkv.at[:, 0:ROWS * (TARGETS - 1), :], s_p1)
        arrived(ga_r.at[0:ROWS * (TARGETS - 1), :], s_p3)
        arrived(ob.at[0:others, :], s_p2)
        arrived(dbuf.at[:, 0:others, :], s_p4)

    @pl.when(jnp.logical_not(works))
    def _():
        arrived(qkv.at[:, 0:ROWS * TARGETS, :], s_p1)
        arrived(ga_r.at[0:ROWS * TARGETS, :], s_p3)


    def sent_x(i):
        @pl.when(i != x)
        def _():
            w_x(i, 0).wait_send()
            w_x(i, 1).wait_send()
            rs2_copy(i).wait_send()

        rs1_copy(i).wait_send()

    loop(4, sent_x)
    loop(8, lambda i: w_sib(i).wait_send())
    for src, buf, base in ((hb, halo, 0), (gcb, ghalo, 12)):
        loop(col_tiles, lambda i: edges_do(src, buf, base, i, lambda copy: copy.wait_send()))


def finish(
    bo, gi, gq, gk, gv, gw_ref, gt_ref, bo_o, gi_o, gq_o, gk_o, gv_o, gw_o, gt_o,
    bo_v, gi_v, gq_v, gk_v, gv_v, gw_v, gt_v, in_sems, out_sems,
):
    held = (bo_v, gi_v, gq_v, gk_v, gv_v, gw_v, gt_v)
    outs = (bo_o, gi_o, gq_o, gk_o, gv_o, gw_o, gt_o)
    loads = [pltpu.make_async_copy(a, b, in_sems.at[i]) for i, (a, b) in enumerate(zip((bo, gi, gq, gk, gv), held))]
    stores = [pltpu.make_async_copy(a, b, out_sems.at[i]) for i, (a, b) in enumerate(zip(held, outs))]
    for load in loads:
        load.start()
    gw_v[...] = gw_ref[0:24, 0:96]
    stores[5].start()
    wide = jnp.concatenate([gt_ref[...], jnp.zeros((112, 128), F32)], axis=0).T
    gt_v[...] = jnp.concatenate([wide[32 * k:32 * k + TAPS, 0:16] for k in range(3)], axis=1)
    stores[6].start()
    for load, store in zip(loads, stores):
        load.wait()
        store.start()
    for store in stores:
        store.wait()


def per_device(frame_input, queries, key_proj, value_proj, out_weight, conv_weight, lengths, grad_output):
    vmem = pl.BlockSpec(memory_space=pltpu.VMEM)
    hbm = pl.BlockSpec(memory_space=pltpu.HBM)
    dma = lambda n: pltpu.SemaphoreType.DMA((n,))
    scratch = [
        ((2, ROWS, D), BF), ((2, ROWS, D), BF),
        ((3, FRAMES, 128), BF), ((2, FRAMES, 128), BF), ((2, FRAMES, 128), BF), ((128, FRAMES), BF),
        ((128, FRAMES), BF), ((2, FRAMES, FRAMES), BF), ((2, FRAMES, FRAMES), BF),
        ((FRAMES, 128), BF), ((2, PAIRS, ROWS, 128), BF), ((2 * ROWS, HD), BF), ((2, PAIRS, ROWS, 128), BF),
        ((FRAMES, 128), BF), ((3, FRAMES, 128), BF), ((3, 2, PAIRS, ROWS, 128), BF),
        ((2, N_DP, 32, 128), BF), ((32, D), F32), ((D, HD), BF), ((32, 128), BF),
        ((2, ROWS, D), F32), ((2, ROWS, D), BF), ((2, 2, 16, D), BF), ((2, 96, D), F32),
        ((2, ROWS, D), BF), ((2, 2, 16, D), BF), ((2, 96, D), F32), ((128, D), F32),
        ((8, 2, 96, HD), BF), ((8, 96, HD), BF), ((4, 2, 96, HD), BF), ((4, 2, 96, HD), BF),
        ((2, 96, HD), F32), ((128, HD), F32),
        ((2, N_DP, 32, 128), BF), ((8, 2, 4, 32, 128), BF), ((2, 4, 32, 128), BF), ((2, 4, 32, 128), BF),
        ((N_DP, 16, 128), BF), ((8, 4, 16, 128), BF), ((4, 16, 128), BF), ((4, 16, 128), BF),
        ((16, 128), BF), ((N_CTX, 16, 128), BF),
    ]
    one = pltpu.SemaphoreType.DMA
    sems = [
        dma(2), one, dma(3), one, one, one, dma(8), dma(17), dma(16), one, one, dma(24), dma(24), one, one, one,
        dma(3), dma(4), dma(4), dma(4), dma(4), one, one, one, one, one, one, one, one, one, one,
    ]
    shapes = (
        ((2, ROWS, D), BF), ((2, ROWS, D), BF), ((2, ROWS, HD), BF), ((2, ROWS, HD), BF), ((2, ROWS, HD), BF),
        ((32, 128), F32), ((16, 128), F32),
    )
    bo, gi, gq, gk, gv, gw, gt = pl.pallas_call(
        kernel,
        out_shape=[jax.ShapeDtypeStruct(s, t) for s, t in shapes],
        in_specs=[pl.BlockSpec(memory_space=pltpu.SMEM)] + [hbm] * 4 + [vmem, vmem, hbm],
        out_specs=[vmem] * 7,
        scratch_shapes=[pltpu.VMEM(s, t) for s, t in scratch] + sems,
        compiler_params=pltpu.CompilerParams(
            collective_id=0, has_side_effects=True, vmem_limit_bytes=60 * 1024 * 1024
        ),
        cost_estimate=pl.CostEstimate(flops=3 * 10**9, bytes_accessed=4 * 10**6, transcendentals=2 * 10**6),
    )(lengths, frame_input, queries, key_proj, value_proj, out_weight.T, conv_weight, grad_output)
    final = shapes[0:5] + (((24, 96), F32), ((TAPS, 48), F32))
    bo, gi, gq, gk, gv, gw, gt = (
        pl.pallas_call(
            finish,
            out_shape=[jax.ShapeDtypeStruct(s, t) for s, t in final],
            in_specs=[hbm] * 5 + [vmem] * 2,
            out_specs=[hbm] * 7,
            scratch_shapes=[pltpu.VMEM(s, t) for s, t in final] + [dma(5), dma(7)],
            compiler_params=pltpu.CompilerParams(vmem_limit_bytes=60 * 1024 * 1024),
            cost_estimate=pl.CostEstimate(flops=10**5, bytes_accessed=3 * 10**6, transcendentals=0),
        )(bo, gi, gq, gk, gv, gw, gt)
    )
    return bo, gi, gq, gk, gv, gw.T, gt


def solution(mesh):
    rows = P("dp", "ctx", None)
    return jax.shard_map(
        per_device,
        mesh=mesh,
        in_specs=(rows, rows, rows, rows, P("ctx", "dp"), P(None, "dp"), P("dp"), rows),
        out_specs=(rows, rows, rows, rows, rows, P("ctx", "dp"), P(None, "dp")),
        check_vma=False,
    )
```

```python
import jax
import jax.numpy as jnp
from jax import lax
from jax.experimental import pallas as pl
from jax.experimental.pallas import tpu as pltpu
from jax.sharding import PartitionSpec as P

BF = jnp.bfloat16
F32 = jnp.float32
N_CTX = 16
N_DP = 32
ROWS = 64
FRAMES = 1024
D = 1536
HD = 768
PAIRS = 6
TARGETS = 2 * PAIRS
TAPS = 31
TILE = 256
CONV_BLOCKS = D // 128
NT = (((1,), (1,)), ((), ()))
TN = (((0,), (0,)), ((), ()))


def target_of(n):
    u, p = n // PAIRS, n % PAIRS
    hi = p // 4
    x = (1 - hi) * p + hi * (2 * (p - 4) + u)
    return 4 * x + 2 * u + hi


def remote(src, dst, send, recv, **axis):
    return pltpu.make_async_remote_copy(
        src_ref=src,
        dst_ref=dst,
        send_sem=send,
        recv_sem=recv,
        device_id=axis,
        device_id_type=pl.DeviceIdType.MESH,
    )


def arrived(dst, sem):
    pltpu.make_async_copy(dst, dst, sem).wait()


def loop(count, body):
    def step(i, carry):
        body(i)
        return carry

    lax.fori_loop(0, count, step, 0)


def mo(value, unit):
    return pl.multiple_of(value, unit)


def kernel(
    len_ref, x_ref, q_ref, k_ref, v_ref, wt_ref, cw_ref, go_ref,
    bo_ref, gi_ref, gq_ref, gk_ref, gv_ref, gw_ref, gt_ref,
    x_v, go_v, qkv, kx, qm, kt, vt, pt, ds, ob, att_r, att, ga_s, ga_r, dbuf, grad_r,
    w_a, taps, w_full, msg_ref,
    hid, hb, halo, hp, gcb, ghalo, gp, tgs,
    pp, rs1, rs2s, rs2, own2, own3, ms, zr, ys, yr, tms, tzr, tys, tyr, th, tr,
    s_in, s_p1, r_p1, s_ay, r_ay, s_az, r_az, s_w, r_w, s_p2, r_p2, s_h, r_h, s_p3, r_p3, s_p4, r_p4,
    s_rs1, r_rs1, s_rs2, r_rs2, s_dp, r_dp, s_de, r_de, s_td, r_td, s_te, r_te, s_t, r_t,
):
    me = lax.axis_index("ctx")
    dp = lax.axis_index("dp")
    x = me // 4
    yh = (me // 2) % 2
    core = me % 2
    sib = 4 * x + 2 * yh + (1 - core)
    ypart = 4 * x + 2 * (1 - yh) + core
    pair = (1 - core) * x + core * (4 + x // 2)
    works = (core * ((x + yh) % 2)) == 0
    zi, yl = dp // 4, dp % 4
    my_rows = pl.ds(mo(me * ROWS, ROWS), ROWS)
    inputs = (q_ref, k_ref, v_ref)

    loads = [pltpu.make_async_copy(a, b, s_in.at[i]) for i, (a, b) in enumerate(((x_ref, x_v), (go_ref, go_v)))]
    for load in loads:
        load.start()

    wide = jnp.concatenate([cw_ref[...].astype(F32), jnp.zeros((TAPS, 80), F32)], axis=1)
    right = jnp.concatenate([wide, jnp.zeros((128 - TAPS, 128), F32)], axis=0).T[0:48, 0:32]
    top = jnp.concatenate([wt_ref[...].astype(F32), right[0:24]], axis=1)
    low = jnp.concatenate([right[24:32], right[32:40], right[40:48], jnp.zeros((8, 32), F32)], axis=1)
    msg_ref[...] = jnp.concatenate([top, low], axis=0).astype(BF)

    barrier = pltpu.get_barrier_semaphore()

    def greet_ctx(i):
        @pl.when(i != me)
        def _():
            pl.semaphore_signal(barrier, inc=1, device_id={"ctx": i}, device_id_type=pl.DeviceIdType.MESH)

    def z_peer(i):
        return 4 * lax.rem(zi + 1 + i, 8) + yl

    def y_peer(i):
        return 4 * zi + lax.rem(yl + 1 + i, 4)

    def ring_peer(i):
        o = lax.rem(4 * yh + yl + 1 + i, 8)
        return o // 4, o % 4, {"ctx": 4 * x + 2 * (o // 4) + core, "dp": 4 * zi + o % 4}

    def greet(to):
        pl.semaphore_signal(barrier, inc=1, device_id=to, device_id_type=pl.DeviceIdType.MESH)

    loop(N_CTX, greet_ctx)
    loop(7, lambda i: greet({"dp": z_peer(i)}))
    loop(7, lambda i: greet(ring_peer(i)[2]))
    pl.semaphore_wait(barrier, N_CTX - 1 + 7 + 7)

    def p1_parts(a, n):
        src = inputs[a].at[n // PAIRS, :, pl.ds(mo((n % PAIRS) * 128, 128), 128)]
        return src, qkv.at[a, my_rows, :]

    def p1_copy(a, n):
        src, dst = p1_parts(a, n)
        return remote(src, dst, s_p1, r_p1.at[a], ctx=target_of(n))

    def p1_start(a):
        def one(i):
            n = lax.rem(i + me, TARGETS)
            t = target_of(n)

            @pl.when(t != me)
            def _():
                p1_copy(a, n).start()

            @pl.when(t == me)
            def _():
                src, dst = p1_parts(a, n)
                pltpu.make_async_copy(src, dst, r_p1.at[a]).start()

        loop(TARGETS, one)

    four = pl.ds(4 * zi, 4)

    def a_y(i):
        remote(msg_ref, w_a.at[yh, dp], s_ay, r_ay, **ring_peer(i)[2]).start()

    def a_z(i):
        remote(w_a.at[:, four], w_a.at[:, four], s_az, r_az.at[zi], dp=z_peer(i)).start()

    def a_z_take(i):
        source = lax.rem(zi + 1 + i, 8)
        arrived(w_a.at[:, pl.ds(4 * source, 4)], r_az.at[source])

    loop(7, a_y)
    pltpu.make_async_copy(msg_ref, w_a.at[yh, dp], r_ay).start()
    p1_start(1)
    arrived(w_a.at[:, four], r_ay)
    loop(7, a_z)
    p1_start(0)
    p1_start(2)
    tgs[...] = jnp.zeros_like(tgs)
    own3[...] = jnp.zeros_like(own3)
    loop(7, a_z_take)
    for y in range(2):
        pieces = w_a[y].astype(F32)
        block = pieces[:, 0:24, :].reshape(HD, 128).T
        w_full[pl.ds(mo((4 * x + 2 * y + core) * 96, 32), 96), :] = block[0:96, :].astype(BF)
        if y == 0:
            rest = pieces[:, 24:32, :].reshape(N_DP * 8, 128)
            moved_rest = [pltpu.roll(rest, 96 - 32 * k, 1).reshape(N_DP, 8, 128) for k in range(3)]
            taps[...] = jnp.concatenate([pieces[:, 0:24, :]] + moved_rest, axis=1).reshape(D, 128).T[96:128, :]

    def w_rows(c):
        return w_full.at[pl.ds(mo(c * 96, 32), 96), :]

    def w_copy(c, slot, to):
        return remote(w_rows(c), w_rows(c), s_w.at[slot], r_w.at[c], ctx=to)

    def w_x(i, y):
        return w_copy(4 * x + 2 * y + core, 1 + 4 * y + i, 4 * i + 2 * yh + core)

    def w_sib(i):
        return w_copy(2 * i + core, 9 + i, sib)

    def w_x_start(y):
        def one(i):
            @pl.when(i != x)
            def _():
                w_x(i, y).start()

        loop(4, one)

    w_x_start(0)
    w_x_start(1)

    lane = lax.broadcasted_iota(jnp.int32, (FRAMES, 128), 1)

    def p1_take(a):
        arrived(qkv.at[a], r_p1.at[a])

    @pl.when(works)
    def _():
        p1_take(1)
        row = lax.broadcasted_iota(jnp.int32, (FRAMES, 128), 0)
        bias = jnp.where(row < len_ref[yh], 0.0, -1e30)
        k = qkv[1].astype(F32)
        for h in range(2):
            kx[h] = jnp.where(lane == 64 * (1 - h), bias, k).astype(BF)
        kt[...] = k.T.astype(BF)
        p1_take(0)
        q = qkv[0].astype(F32) * 0.125
        for h in range(2):
            mine = (lane // 64) == h
            qm[h] = jnp.where(mine, q, jnp.where(lane == 64 * (1 - h), 1.0, 0.0)).astype(BF)

    def weights_of(h):
        @pl.when(works)
        def _():
            def tile(i):
                cols = pl.ds(mo(i * TILE, TILE), TILE)
                s = lax.dot_general(kx[h], qm[h, cols, :], NT, preferred_element_type=F32)
                e = jnp.exp(s - jnp.max(s, axis=0, keepdims=True))
                pt[h, :, cols] = (e * (1.0 / jnp.sum(e, axis=0, keepdims=True))).astype(BF)

            loop(FRAMES // TILE, tile)

    weights_of(0)
    weights_of(1)

    def p2_copy(c):
        rows = pl.ds(mo(c * ROWS, ROWS), ROWS)
        return remote(ob.at[rows, :], att_r.at[yh, pair], s_p2, r_p2, ctx=c)

    def p2_start(c):
        @pl.when(c != me)
        def _():
            p2_copy(c).start()

        @pl.when(c == me)
        def _():
            pltpu.make_async_copy(ob.at[my_rows, :], att_r.at[yh, pair], r_p2).start()

    @pl.when(works)
    def _():
        p1_take(2)
        vt[...] = qkv[2].astype(F32).T.astype(BF)

        def tile(i):
            cols = pl.ds(mo(i * TILE, TILE), TILE)
            out = [
                jnp.dot(vt[64 * h:64 * h + 64, :], pt[h, :, cols], preferred_element_type=F32) for h in range(2)
            ]
            ob[cols, :] = jnp.concatenate(out, axis=0).T.astype(BF)
            loop(TILE // ROWS, lambda j: p2_start(i * (TILE // ROWS) + j))

        loop(FRAMES // TILE, tile)

    def w_forward(i):
        c = 2 * i + core

        @pl.when(((c - me) * (c - ypart)) != 0)
        def _():
            arrived(w_rows(c), r_w.at[c])

        w_sib(i).start()

    loop(8, w_forward)

    def w_last(i):
        c = 2 * i + (1 - core)
        arrived(w_rows(c), r_w.at[c])

    loop(8, w_last)
    arrived(att_r, r_p2)
    for u in range(2):
        for p in range(PAIRS):
            att[64 * u:64 * u + 64, 128 * p:128 * p + 128] = att_r[u, p]

    frame = lax.broadcasted_iota(jnp.int32, (ROWS, TILE), 0) + me * ROWS
    before, after = me > 0, me < N_CTX - 1
    col_tiles = D // TILE

    def edge_copies(src, buf, base, i):
        cols = pl.ds(mo(i * TILE, TILE), TILE)
        up = remote(
            src.at[:, 48:64, cols], buf.at[0, :, :, cols], s_h.at[base + i], r_h.at[base + i],
            ctx=lax.rem(me + 1, N_CTX),
        )
        down = remote(
            src.at[:, 0:16, cols], buf.at[1, :, :, cols], s_h.at[base + 6 + i], r_h.at[base + 6 + i],
            ctx=lax.rem(me + N_CTX - 1, N_CTX),
        )
        return up, down

    def edges_do(src, buf, base, i, what):
        up, down = edge_copies(src, buf, base, i)

        @pl.when(after)
        def _():
            what(up)

        @pl.when(before)
        def _():
            what(down)

    def edges_take(buf, base, padded, i):
        cols = pl.ds(mo(i * TILE, TILE), TILE)
        for side, first, inner in ((0, 0, before), (1, 80, after)):
            @pl.when(inner)
            def _():
                arrived(buf.at[side, :, :, cols], r_h.at[base + 6 * side + i])
                padded[:, first:first + 16, cols] = buf[side, :, :, cols].astype(F32)

            @pl.when(jnp.logical_not(inner))
            def _():
                padded[:, first:first + 16, cols] = jnp.zeros((2, 16, TILE), F32)

    def rolled_by(block, r):
        return block if r == 0 else pltpu.roll(block, 96 - r, 0)

    for load in loads:
        load.wait()

    def project(i):
        cols = pl.ds(mo(i * TILE, TILE), TILE)
        out = lax.dot_general(att[...], w_full[cols, :], NT, preferred_element_type=F32)
        for u in range(2):
            h = (out[64 * u:64 * u + 64, :] + x_v[u, :, cols].astype(F32)).astype(BF).astype(F32)
            masked = jnp.where(frame < len_ref[u], h, 0.0)
            hid[u, :, cols] = h
            hb[u, :, cols] = masked.astype(BF)
            hp[u, 16:80, cols] = masked
        edges_do(hb, halo, 0, i, lambda copy: copy.start())

    loop(col_tiles, project)

    def conv_forward(i):
        edges_take(halo, 0, hp, i)
        for half in range(2):
            cols = pl.ds(mo(i * TILE + half * 128, 128), 128)
            w = taps[:, cols]
            for u in range(2):
                block = hp[u, :, cols]
                acc = jnp.zeros((ROWS, 128), F32)
                for r in range(8):
                    moved = rolled_by(block, r)
                    for a in range(4):
                        j = 8 * a + r - 1
                        if 0 <= j < TAPS:
                            acc = acc + w[j:j + 1, :] * moved[8 * a:8 * a + ROWS, :]
                sg = jax.nn.sigmoid(acc)
                bo_ref[u, :, cols] = (hid[u, :, cols] + acc * sg).astype(BF)
                gc = (go_v[u, :, cols].astype(F32) * (sg * (1.0 + acc * (1.0 - sg)))).astype(BF)
                gcb[u, :, cols] = gc
                gp[u, 16:80, cols] = gc.astype(F32)
        edges_do(gcb, ghalo, 12, i, lambda copy: copy.start())

    loop(col_tiles, conv_forward)

    def taps_gradient(i):
        cols = pl.ds(mo(i * 128, 128), 128)
        blocks = [hp[u, :, cols] for u in range(2)]
        grads = [gp[u, 16:80, cols] for u in range(2)]
        for r in range(8):
            moved = [rolled_by(block, r) for block in blocks]
            for a in range(4):
                j = 8 * a + r - 1
                if 0 <= j < TAPS:
                    total = sum(g * m[8 * a:8 * a + ROWS, :] for g, m in zip(grads, moved))
                    tgs[j:j + 1, cols] = jnp.sum(total, axis=0, keepdims=True)

    frame_c = lax.broadcasted_iota(jnp.int32, (ROWS, 128), 0) + me * ROWS

    def conv_backward(i):
        edges_take(ghalo, 12, gp, i)
        for half in range(2):
            cols = pl.ds(mo(i * TILE + half * 128, 128), 128)
            w = taps[:, cols]
            for u in range(2):
                block = gp[u, :, cols]
                acc = jnp.zeros((ROWS, 128), F32)
                for r in range(8):
                    moved = rolled_by(block, r)
                    for a in range(4):
                        j = 31 - (8 * a + r)
                        if 0 <= j < TAPS:
                            acc = acc + w[j:j + 1, :] * moved[8 * a:8 * a + ROWS, :]
                gi = go_v[u, :, cols].astype(F32) + jnp.where(frame_c < len_ref[u], acc, 0.0)
                gi_ref[u, :, cols] = gi.astype(BF)

    loop(col_tiles, conv_backward)

    def p3_copy(n):
        return remote(
            ga_s.at[n // PAIRS, n % PAIRS], ga_r.at[my_rows, :], s_p3, r_p3, ctx=target_of(n)
        )

    gi_rows = gi_ref[...].reshape(2 * ROWS, D)

    def p3_start(n):
        t = target_of(n)

        @pl.when(t != me)
        def _():
            p3_copy(n).start()

        @pl.when(t == me)
        def _():
            pltpu.make_async_copy(ga_s.at[n // PAIRS, n % PAIRS], ga_r.at[my_rows, :], r_p3).start()

    def cotangent(i):
        cols = pl.ds(mo(i * TILE, TILE), TILE)
        out = jnp.dot(gi_rows, w_full[:, cols], preferred_element_type=F32).astype(BF)
        for u in range(2):
            for half in range(2):
                ga_s[u, 2 * i + half] = out[64 * u:64 * u + 64, 128 * half:128 * half + 128]
        loop(4, lambda m: p3_start((m // 2) * PAIRS + 2 * i + m % 2))

    loop(HD // TILE, cotangent)

    def over_dp(src, zr, ys, yr, s_z, r_z, s_y, r_y):
        def first(i):
            to = z_peer(i)
            remote(src.at[pl.ds(to - yl, 4)], zr.at[zi], s_z, r_z, dp=to).start()

        def start():
            loop(7, first)
            pltpu.make_async_copy(src.at[four], zr.at[zi], r_z).start()

        def second(i):
            to = y_peer(i)
            remote(ys.at[to - 4 * zi], yr.at[yl], s_y, r_y, dp=to).start()

        def turn():
            arrived(zr, r_z)
            ys[...] = jnp.sum(zr[...].astype(F32), axis=0).astype(BF)
            loop(3, second)
            pltpu.make_async_copy(ys.at[yl], yr.at[yl], r_y).start()

        def end():
            arrived(yr, r_y)
            return jnp.sum(yr[...].astype(F32), axis=0)

        def sent():
            arrived(src.at[0:28], s_z)
            arrived(ys.at[0:3], s_y)

        return start, turn, end, sent

    td_start, td_turn, td_end, td_sent = over_dp(tms, tzr, tys, tyr, s_td, r_td, s_te, r_te)

    def dp_first(i):
        remote(ms.at[:, lax.rem(zi + 1 + i, 8)], zr.at[zi], s_dp, r_dp, dp=z_peer(i)).start()

    def dp_start():
        loop(7, dp_first)
        pltpu.make_async_copy(ms.at[:, zi], zr.at[zi], r_dp).start()

    def dp_second(i):
        yh_to, yl_to, to = ring_peer(i)
        remote(ys.at[yh_to, yl_to], yr.at[yh, yl], s_de, r_de, **to).start()

    def dp_turn():
        arrived(zr, r_dp)
        summed = jnp.sum(zr[...].astype(F32), axis=0).reshape(2, 4, 24, 128)
        ys[...] = jnp.concatenate([summed, jnp.zeros((2, 4, 8, 128), F32)], axis=2).astype(BF)
        loop(7, dp_second)
        pltpu.make_async_copy(ys.at[yh, yl], yr.at[yh, yl], r_de).start()

    def rs1_copy(i):
        return remote(
            pp.at[pl.ds(2 * i, 2), 1 - core], rs1.at[pl.ds(2 * i, 2)], s_rs1.at[i], r_rs1.at[i], ctx=sib
        )

    def panel(i):
        cols = pl.ds(mo(i * 384, 128), 384)
        gi_cols = jnp.concatenate([gi_ref[0, :, cols], gi_ref[1, :, cols]], axis=0)
        out = lax.dot_general(gi_cols, att[...], TN, preferred_element_type=F32)
        pp[pl.ds(2 * i, 2)] = out.reshape(2, 2, 96, HD).astype(BF)
        rs1_copy(i).start()

    loop(4, panel)
    loop(CONV_BLOCKS, taps_gradient)
    tap_rows = tgs[...].T.reshape(N_DP, 48, 128)
    packed = [tap_rows[:, 0:16, :]] + [
        pltpu.roll(tap_rows[:, 16 * k:16 * k + 16, :].reshape(N_DP * 16, 128), 32 * k, 1).reshape(N_DP, 16, 128)
        for k in (1, 2)
    ]
    tms[...] = (packed[0] + packed[1] + packed[2]).astype(BF)
    td_start()

    def rs2_copy(i):
        return remote(rs2s.at[i], rs2.at[x], s_rs2.at[i], r_rs2.at[x], ctx=4 * i + 2 * yh + core)

    def rs2_start(i):
        two = pl.ds(2 * i, 2)
        arrived(rs1.at[two], r_rs1.at[i])
        total = pp[two, core].astype(F32) + rs1[two].astype(F32)

        @pl.when(i != x)
        def _():
            rs2s[i] = total.astype(BF)
            rs2_copy(i).start()

        @pl.when(i == x)
        def _():
            own2[...] = total

    loop(4, rs2_start)

    def p4_copy(a, c):
        rows = pl.ds(mo(c * ROWS, ROWS), ROWS)
        return remote(
            dbuf.at[a, rows, :], grad_r.at[a, yh, pair], s_p4, r_p4.at[a], ctx=c,
        )

    def p4_start(a, i):
        def one(j):
            c = i * (TILE // ROWS) + j

            @pl.when(c != me)
            def _():
                p4_copy(a, c).start()

            @pl.when(c == me)
            def _():
                pltpu.make_async_copy(dbuf.at[a, my_rows, :], grad_r.at[a, yh, pair], r_p4.at[a]).start()

        loop(TILE // ROWS, one)

    tile_lane = lax.broadcasted_iota(jnp.int32, (TILE, 128), 1) // 64

    @pl.when(works)
    def _():
        arrived(ga_r, r_p3)

        def values(i):
            rows = pl.ds(mo(i * TILE, TILE), TILE)
            first = jnp.dot(pt[0, rows, :], ga_r[...], preferred_element_type=F32)
            second = jnp.dot(pt[1, rows, :], ga_r[...], preferred_element_type=F32)
            dbuf[2, rows, :] = jnp.where(tile_lane == 0, first, second).astype(BF)
            p4_start(2, i)

        loop(FRAMES // TILE, values)

    def backward_tile(i):
        cols = pl.ds(mo(i * TILE, TILE), TILE)
        ga = ga_r[cols, :].astype(F32)
        prod = (ga * ob[cols, :].astype(F32)).T
        parts = []
        for h in range(2):
            gmb = jnp.where(tile_lane == h, ga, 0.0).astype(BF)
            delta = jnp.sum(prod[64 * h:64 * h + 64, :], axis=0, keepdims=True)
            dpt = lax.dot_general(qkv[2], gmb, NT, preferred_element_type=F32)
            dst = (pt[h, :, cols].astype(F32) * (dpt - delta)).astype(BF)
            ds[h, :, cols] = dst
            parts.append(jnp.dot(kt[64 * h:64 * h + 64, :], dst, preferred_element_type=F32))
        dbuf[0, cols, :] = (jnp.concatenate(parts, axis=0).T * 0.125).astype(BF)
        p4_start(0, i)

    def backward_half(first):
        @pl.when(works)
        def _():
            loop(2, lambda i: backward_tile(i + first))

    td_turn()

    def rs2_take(i):
        @pl.when(i != x)
        def _():
            arrived(rs2.at[i], r_rs2.at[i])
            own2[...] += rs2[i].astype(F32)

    loop(4, rs2_take)
    for y in range(2):
        own3[0:96, :] = own2[y]
        ms[y] = own3[...].T.reshape(8, 96, 128).astype(BF)
    dp_start()
    backward_half(0)

    def t_copy(c):
        return remote(th, tr.at[me], s_t, r_t, ctx=c)

    def t_start(i):
        t_copy(lax.rem(i + 1 + me, N_CTX)).start()

    th[...] = td_end().astype(BF)
    loop(N_CTX - 1, t_start)
    pltpu.make_async_copy(th, tr.at[me], r_t).start()
    backward_half(2)

    @pl.when(works)
    def _():
        for h in range(2):
            qm[h] = jnp.where((lane // 64) == h, qkv[0].astype(F32) * 0.125, 0.0).astype(BF)

        def keys(i):
            rows = pl.ds(mo(i * TILE, TILE), TILE)
            out = jnp.dot(ds[0, rows, :], qm[0], preferred_element_type=F32)
            out = out + jnp.dot(ds[1, rows, :], qm[1], preferred_element_type=F32)
            dbuf[1, rows, :] = out.astype(BF)
            p4_start(1, i)

        loop(FRAMES // TILE, keys)

    dp_turn()

    def p4_take(a):
        arrived(grad_r.at[a], r_p4.at[a])

    for a, out in ((2, gv_ref), (0, gq_ref), (1, gk_ref)):
        p4_take(a)
        for u in range(2):
            for p in range(PAIRS):
                out[u, :, 128 * p:128 * p + 128] = grad_r[a, u, p]

    arrived(tr, r_t)
    gt_ref[...] = jnp.sum(tr[...].astype(F32), axis=0)
    arrived(yr, r_de)
    gw_ref[...] = jnp.sum(yr[...].astype(F32).reshape(8, 32, 128), axis=0)

    arrived(w_a.at[0, 0:7], s_ay)
    arrived(w_a.at[:, 0:28], s_az)
    td_sent()
    arrived(zr.at[0:7], s_dp)
    arrived(w_a.at[0, 0:7], s_de)
    arrived(tr.at[0:N_CTX - 1], s_t)
    others = ROWS * (N_CTX - 1)

    @pl.when(works)
    def _():
        arrived(qkv.at[:, 0:ROWS * (TARGETS - 1), :], s_p1)
        arrived(ga_r.at[0:ROWS * (TARGETS - 1), :], s_p3)
        arrived(ob.at[0:others, :], s_p2)
        arrived(dbuf.at[:, 0:others, :], s_p4)

    @pl.when(jnp.logical_not(works))
    def _():
        arrived(qkv.at[:, 0:ROWS * TARGETS, :], s_p1)
        arrived(ga_r.at[0:ROWS * TARGETS, :], s_p3)


    def sent_x(i):
        @pl.when(i != x)
        def _():
            w_x(i, 0).wait_send()
            w_x(i, 1).wait_send()
            rs2_copy(i).wait_send()

        rs1_copy(i).wait_send()

    loop(4, sent_x)
    loop(8, lambda i: w_sib(i).wait_send())
    for src, buf, base in ((hb, halo, 0), (gcb, ghalo, 12)):
        loop(col_tiles, lambda i: edges_do(src, buf, base, i, lambda copy: copy.wait_send()))


def finish(
    bo, gi, gq, gk, gv, gw_ref, gt_ref, bo_o, gi_o, gq_o, gk_o, gv_o, gw_o, gt_o,
    bo_v, gi_v, gq_v, gk_v, gv_v, gw_v, gt_v, in_sems, out_sems,
):
    held = (bo_v, gi_v, gq_v, gk_v, gv_v, gw_v, gt_v)
    outs = (bo_o, gi_o, gq_o, gk_o, gv_o, gw_o, gt_o)
    loads = [pltpu.make_async_copy(a, b, in_sems.at[i]) for i, (a, b) in enumerate(zip((bo, gi, gq, gk, gv), held))]
    stores = [pltpu.make_async_copy(a, b, out_sems.at[i]) for i, (a, b) in enumerate(zip(held, outs))]
    for load in loads:
        load.start()
    gw_v[...] = gw_ref[0:24, 0:96]
    stores[5].start()
    wide = jnp.concatenate([gt_ref[...], jnp.zeros((112, 128), F32)], axis=0).T
    gt_v[...] = jnp.concatenate([wide[32 * k:32 * k + TAPS, 0:16] for k in range(3)], axis=1)
    stores[6].start()
    for load, store in zip(loads, stores):
        load.wait()
        store.start()
    for store in stores:
        store.wait()


def per_device(frame_input, queries, key_proj, value_proj, out_weight, conv_weight, lengths, grad_output):
    vmem = pl.BlockSpec(memory_space=pltpu.VMEM)
    hbm = pl.BlockSpec(memory_space=pltpu.HBM)
    dma = lambda n: pltpu.SemaphoreType.DMA((n,))
    scratch = [
        ((2, ROWS, D), BF), ((2, ROWS, D), BF),
        ((3, FRAMES, 128), BF), ((2, FRAMES, 128), BF), ((2, FRAMES, 128), BF), ((128, FRAMES), BF),
        ((128, FRAMES), BF), ((2, FRAMES, FRAMES), BF), ((2, FRAMES, FRAMES), BF),
        ((FRAMES, 128), BF), ((2, PAIRS, ROWS, 128), BF), ((2 * ROWS, HD), BF), ((2, PAIRS, ROWS, 128), BF),
        ((FRAMES, 128), BF), ((3, FRAMES, 128), BF), ((3, 2, PAIRS, ROWS, 128), BF),
        ((2, N_DP, 32, 128), BF), ((32, D), F32), ((D, HD), BF), ((32, 128), BF),
        ((2, ROWS, D), F32), ((2, ROWS, D), BF), ((2, 2, 16, D), BF), ((2, 96, D), F32),
        ((2, ROWS, D), BF), ((2, 2, 16, D), BF), ((2, 96, D), F32), ((128, D), F32),
        ((8, 2, 96, HD), BF), ((8, 96, HD), BF), ((4, 2, 96, HD), BF), ((4, 2, 96, HD), BF),
        ((2, 96, HD), F32), ((128, HD), F32),
        ((2, 8, 96, 128), BF), ((8, 2, 96, 128), BF), ((2, 4, 32, 128), BF), ((2, 4, 32, 128), BF),
        ((N_DP, 16, 128), BF), ((8, 4, 16, 128), BF), ((4, 16, 128), BF), ((4, 16, 128), BF),
        ((16, 128), BF), ((N_CTX, 16, 128), BF),
    ]
    one = pltpu.SemaphoreType.DMA
    sems = [
        dma(2), one, dma(3), one, one, one, dma(8), dma(17), dma(16), one, one, dma(24), dma(24), one, one, one,
        dma(3), dma(4), dma(4), dma(4), dma(4), one, one, one, one, one, one, one, one, one, one,
    ]
    shapes = (
        ((2, ROWS, D), BF), ((2, ROWS, D), BF), ((2, ROWS, HD), BF), ((2, ROWS, HD), BF), ((2, ROWS, HD), BF),
        ((32, 128), F32), ((16, 128), F32),
    )
    bo, gi, gq, gk, gv, gw, gt = pl.pallas_call(
        kernel,
        out_shape=[jax.ShapeDtypeStruct(s, t) for s, t in shapes],
        in_specs=[pl.BlockSpec(memory_space=pltpu.SMEM)] + [hbm] * 4 + [vmem, vmem, hbm],
        out_specs=[vmem] * 7,
        scratch_shapes=[pltpu.VMEM(s, t) for s, t in scratch] + sems,
        compiler_params=pltpu.CompilerParams(
            collective_id=0, has_side_effects=True, vmem_limit_bytes=60 * 1024 * 1024
        ),
        cost_estimate=pl.CostEstimate(flops=3 * 10**9, bytes_accessed=4 * 10**6, transcendentals=2 * 10**6),
    )(lengths, frame_input, queries, key_proj, value_proj, out_weight.T, conv_weight, grad_output)
    final = shapes[0:5] + (((24, 96), F32), ((TAPS, 48), F32))
    bo, gi, gq, gk, gv, gw, gt = (
        pl.pallas_call(
            finish,
            out_shape=[jax.ShapeDtypeStruct(s, t) for s, t in final],
            in_specs=[hbm] * 5 + [vmem] * 2,
            out_specs=[hbm] * 7,
            scratch_shapes=[pltpu.VMEM(s, t) for s, t in final] + [dma(5), dma(7)],
            compiler_params=pltpu.CompilerParams(vmem_limit_bytes=60 * 1024 * 1024),
            cost_estimate=pl.CostEstimate(flops=10**5, bytes_accessed=3 * 10**6, transcendentals=0),
        )(bo, gi, gq, gk, gv, gw, gt)
    )
    return bo, gi, gq, gk, gv, gw.T, gt


def solution(mesh):
    rows = P("dp", "ctx", None)
    return jax.shard_map(
        per_device,
        mesh=mesh,
        in_specs=(rows, rows, rows, rows, P("ctx", "dp"), P(None, "dp"), P("dp"), rows),
        out_specs=(rows, rows, rows, rows, rows, P("ctx", "dp"), P(None, "dp")),
        check_vma=False,
    )
```
